32 devices in a mesh: wide: 8 (over y, x, core), narrow: 4 (over z).
Axes of the slice: x: 2, y: 2, z: 4, core: 2. Of those that a mesh axis runs over, the one named last changes fastest.
Arguments:
- params: float32 [8, 4, 1024, 512], P('wide', 'narrow'), may hold values from -6 to 6
- public: float32 [8, 4, 1024, 512], P('wide', 'narrow'), may hold values from -6 to 6
- mixed: float32 [8, 4, 1024, 512], P('wide', 'narrow'), may hold values from -6 to 6
- inputs: bfloat16 [8, 4, 256, 1024], P('wide', 'narrow'), may hold values from -6 to 6
- cotangent: bfloat16 [8, 4, 256, 512], P('wide', 'narrow'), may hold values from -1.5 to 1.5
- block_ids: int32 [8, 4, 2, 8], P('wide', 'narrow'), may hold values from 0 to 31, as said below
- block_counts: int32 [8, 4, 2], P('wide', 'narrow'), may hold values from 1 to 8, as said below
Outputs:
- params_out: float32 [8, 4, 1024, 512], P('wide', 'narrow')
- public_out: float32 [8, 4, 1024, 512], P('wide', 'narrow')
- mixed_out: float32 [8, 4, 1024, 512], P('wide', 'narrow')
The draws below stay inside these ranges and needn't reach their ends.
Inputs may be any that keep to these rules, and one draw needn't show every extreme that they name: `block_ids`: each row of 8 entries holds distinct tile numbers; entries past the row's count are unused. `block_counts`: some replica uses all 8 entries in some round in every draw.
All inputs are finite; a program needn't handle non-finite values.
Results may differ from the reference program's by a relative error of at most 0.0003.
Values sent between devices are 32-bit elements; how exact they have to be, the bound alone decides.
A program may use at most 128 MiB of HBM per device.

```python
import jax
import jax.numpy as jnp

D = 1024
COLS = 512
TILE = 128
KMAX = 8
ROUNDS = 2
TOK_DEV = 256
WIDE_REPL = 8
NARROW_REPL = 4
BLOCKS = 32


def draw_block_ids(key, part):
    total = WIDE_REPL * NARROW_REPL * ROUNDS
    keys = jax.random.split(key, total)
    orders = jax.vmap(lambda single: jax.random.permutation(single, BLOCKS))(keys)
    return orders[:, :KMAX].astype(jnp.int32).reshape(WIDE_REPL, NARROW_REPL, ROUNDS, KMAX)


def draw_block_counts(key, part):
    total = WIDE_REPL * NARROW_REPL * ROUNDS
    first, second, third = jax.random.split(jax.random.fold_in(key, 7), 3)
    base = jax.random.randint(first, (total,), 1, KMAX // 2 + 1)
    busy = jax.random.randint(second, (total,), 0, 8) == 0
    base = jnp.where(busy, KMAX, base)
    chosen = jax.random.randint(third, (), 0, total)
    base = base.at[chosen].set(KMAX)
    return base.astype(jnp.int32).reshape(WIDE_REPL, NARROW_REPL, ROUNDS)


def level_of(key, dims, pieces, least, high):
    level = 1.0
    for position, shards_of in pieces:
        heights = jax.random.uniform(jax.random.fold_in(jax.random.fold_in(key, 6), position), (shards_of,), jnp.float32, least / len(pieces), high / len(pieces))
        level = level * jnp.repeat(jnp.exp(heights), dims[position] // shards_of).reshape((-1,) + (1,) * (len(dims) - 1 - position))
    return level


def bell_draw(key, extent, scale, bound, cuts=(), kind=jnp.bfloat16):
    array = scale * jax.random.normal(key, extent, jnp.float32)
    if cuts:
        array = array * level_of(key, extent, cuts, -0.22, 0.18)
    return jnp.clip(array, -bound, bound).astype(kind)


def setup_inputs(seed: int = 0) -> dict:
    key_of = jax.random.split(jax.random.key(seed), 8)
    params = bell_draw(key_of[0], (WIDE_REPL, NARROW_REPL, D, COLS), 1.0, 6.0, ((0, 8), (1, 4)), jnp.float32)
    public = bell_draw(key_of[1], (WIDE_REPL, NARROW_REPL, D, COLS), 1.0, 6.0, ((0, 8), (1, 4)), jnp.float32)
    mixed = bell_draw(key_of[2], (WIDE_REPL, NARROW_REPL, D, COLS), 1.0, 6.0, ((0, 8), (1, 4)), jnp.float32)
    inputs = bell_draw(key_of[3], (WIDE_REPL, NARROW_REPL, TOK_DEV, D), 1.0, 6.0, ((0, 8), (1, 4)))
    cotangent = bell_draw(key_of[4], (WIDE_REPL, NARROW_REPL, TOK_DEV, COLS), (4.0 / TOK_DEV ** 0.5), 1.5, ((0, 8), (1, 4)))
    block_ids = draw_block_ids(jax.random.fold_in(key_of[7], 71), 0)
    block_counts = draw_block_counts(jax.random.fold_in(key_of[7], 71), 0)
    return dict(params=params, public=public, mixed=mixed, inputs=inputs, cotangent=cotangent, block_ids=block_ids, block_counts=block_counts)


LEARN_RATE = 0.05
NEIGHBOUR_WEIGHT = 0.2
CONSENSUS = 0.4


def to_blocks(matrix):
    leading = matrix.shape[:-2]
    row_tiles = D // TILE
    col_tiles = COLS // TILE
    shaped = matrix.reshape(leading + (row_tiles, TILE, col_tiles, TILE))
    shaped = jnp.swapaxes(shaped, -3, -2)
    return shaped.reshape(leading + (row_tiles * col_tiles, TILE, TILE))


def from_blocks(blocks):
    leading = blocks.shape[:-3]
    row_tiles = D // TILE
    col_tiles = COLS // TILE
    shaped = blocks.reshape(leading + (row_tiles, col_tiles, TILE, TILE))
    shaped = jnp.swapaxes(shaped, -3, -2)
    return shaped.reshape(leading + (D, COLS))


def pick_one(current, public, listed):
    return current[listed] - public[listed]


def add_one(blocks, listed, values):
    return blocks.at[listed].add(values)


pick_all = jax.vmap(jax.vmap(pick_one))
add_all = jax.vmap(jax.vmap(add_one))


def reference(params, public, mixed, inputs, cotangent, block_ids, block_counts):
    gradient = jnp.einsum("abtd,abtc->abdc", inputs.astype(jnp.float32), cotangent.astype(jnp.float32))
    current = to_blocks(params - LEARN_RATE * gradient)
    public_blocks = to_blocks(public)
    mixed_blocks = to_blocks(mixed)
    slot_index = jnp.arange(KMAX, dtype=jnp.int32)
    for round_index in range(ROUNDS):
        listed = block_ids[:, :, round_index, :]
        in_use = slot_index[None, None, :] < block_counts[:, :, round_index, None]
        packed = jnp.where(in_use[..., None, None], pick_all(current, public_blocks, listed), 0.0)
        public_blocks = add_all(public_blocks, listed, packed)
        mixed_blocks = add_all(mixed_blocks, listed, NEIGHBOUR_WEIGHT * packed)
        for axis_num in (0, 1):
            for offset in (1, -1):
                moved = jnp.roll(packed, offset, axis=axis_num)
                moved_ids = jnp.roll(listed, offset, axis=axis_num)
                mixed_blocks = add_all(mixed_blocks, moved_ids, NEIGHBOUR_WEIGHT * moved)
        current = current + CONSENSUS * (mixed_blocks - public_blocks)
    return from_blocks(current), from_blocks(public_blocks), from_blocks(mixed_blocks)
```

```python
import functools

import jax
import jax.numpy as jnp
from jax import lax
from jax.experimental import pallas as pl
from jax.experimental.pallas import tpu as pltpu
from jax.sharding import PartitionSpec as P

TILE = 128
LEARN_RATE = 0.05
NEIGHBOUR_WEIGHT = 0.2
CONSENSUS = 0.4
CHUNK = 256
SUBLANES = 8
SIDES = 4
MESH = pl.DeviceIdType.MESH


def kernel(
    sizes, rounds, slots, ids, bands, columns, counts, params, public, mixed, inputs, cotangent,
    params_out, public_out, mixed_out,
    acts, cots, cur, pub, mix, maps, map_table, load_sem, map_send, map_recv, table_sem,
    send_sem, recv_sem, out_sem, *buffers
):
    sends, recvs = buffers[:rounds], buffers[rounds:]
    row_tiles, col_tiles = cur.shape[:2]
    rows = row_tiles * TILE
    wide, narrow = lax.axis_index("wide"), lax.axis_index("narrow")
    wide_size, narrow_size = sizes
    partners = (
        (wide, lax.rem(narrow + 1, narrow_size)),
        (wide, lax.rem(narrow + narrow_size - 1, narrow_size)),
        (lax.rem(wide + 1, wide_size), narrow),
        (lax.rem(wide + wide_size - 1, wide_size), narrow),
    )

    load_acts = pltpu.make_async_copy(inputs.at[0, 0], acts, load_sem.at[0])
    load_cots = pltpu.make_async_copy(cotangent.at[0, 0], cots, load_sem.at[1])

    def column_loads(source, held, first):
        return [
            pltpu.make_async_copy(
                source.at[:, :, pl.ds(j * TILE, TILE)], held.at[:, j], load_sem.at[first + j]
            )
            for j in range(col_tiles)
        ]

    load_cur = column_loads(params, cur, 2)
    load_pub = column_loads(public, pub, 2 + col_tiles)
    load_mix = column_loads(mixed, mix, 2 + 2 * col_tiles)
    for load in [load_acts, load_cots] + load_cur + load_pub + load_mix:
        load.start()

    barrier = pltpu.get_barrier_semaphore()
    for partner in partners:
        pl.semaphore_signal(barrier, inc=1, device_id=partner, device_id_type=MESH)

    row = lax.broadcasted_iota(jnp.int32, (SUBLANES, TILE), 0)
    lane = lax.broadcasted_iota(jnp.int32, (SUBLANES, TILE), 1)
    own_map = jnp.full((SUBLANES, TILE), slots, jnp.int32)
    for r in range(rounds):
        for s in range(slots):
            used = jnp.full((SUBLANES, TILE), counts[r], jnp.int32) > s
            own_map = jnp.where((row == r) & (lane == ids[r, s]) & used, s, own_map)
    maps[0] = own_map
    for r in range(rounds):
        sends[r][slots] = jnp.zeros((TILE, TILE), jnp.float32)
        for side in range(SIDES):
            recvs[r][side, slots] = jnp.zeros((TILE, TILE), jnp.float32)

    pl.semaphore_wait(barrier, SIDES)
    map_copies = [
        pltpu.make_async_remote_copy(
            src_ref=maps.at[0], dst_ref=maps.at[1 + side], send_sem=map_send.at[side],
            recv_sem=map_recv.at[side], device_id=partners[side], device_id_type=MESH,
        )
        for side in range(SIDES)
    ]
    for copy in map_copies:
        copy.start()

    def slot_copy(r, side, first, size):
        return pltpu.make_async_remote_copy(
            src_ref=sends[r].at[pl.ds(first, size)],
            dst_ref=recvs[r].at[side, pl.ds(first, size)],
            send_sem=send_sem.at[r, side], recv_sem=recv_sem.at[r, side],
            device_id=partners[side], device_id_type=MESH,
        )

    def arrived(r, tile):
        total = recvs[r][0, map_table[1, r, tile]]
        for side in range(1, SIDES):
            total = total + recvs[r][side, map_table[1 + side, r, tile]]
        return total

    load_acts.wait()
    load_cots.wait()
    for load in load_cur:
        load.wait()
    for first in range(0, rows, CHUNK):
        gradient = lax.dot_general(
            acts[:, first:first + CHUNK], cots[...], (((0,), (0,)), ((), ())),
            preferred_element_type=jnp.float32,
        )
        for j in range(col_tiles):
            for i in range(CHUNK // TILE):
                part = gradient[i * TILE:(i + 1) * TILE, j * TILE:(j + 1) * TILE]
                at = first // TILE + i
                cur[at, j] = cur[at, j] - LEARN_RATE * part
    for load in load_pub:
        load.wait()

    for r in range(rounds):
        for s in range(slots):
            tile = ids[r, s]
            i, j = bands[r, s], columns[r, s]
            value = cur[i, j]
            if r:
                value = value + CONSENSUS * NEIGHBOUR_WEIGHT * arrived(r - 1, tile)
            sends[r][s] = value - pub[i, j]
            for side in range(SIDES):
                slot_copy(r, side, s, 1).start()

        if r == 0:
            for copy in map_copies:
                copy.wait()
            table = pltpu.make_async_copy(maps, map_table, table_sem)
            table.start()
            table.wait()
            for load in load_mix:
                load.wait()

        for j in range(col_tiles):
            def own_part(i, carry):
                tile = i * col_tiles + j
                q = sends[r][map_table[0, r, tile]]
                new_pub = pub[i, j] + q
                new_cur, new_mix = cur[i, j], mix[i, j]
                if r:
                    total = arrived(r - 1, tile)
                    new_cur = new_cur + CONSENSUS * NEIGHBOUR_WEIGHT * total
                    q = q + total
                new_mix = new_mix + NEIGHBOUR_WEIGHT * q
                pub[i, j] = new_pub
                mix[i, j] = new_mix
                cur[i, j] = new_cur + CONSENSUS * (new_mix - new_pub)
                return carry

            lax.fori_loop(0, row_tiles, own_part, 0)

        if r == rounds - 1:
            writes = [
                pltpu.make_async_copy(
                    pub.at[:, j], public_out.at[:, :, pl.ds(j * TILE, TILE)], out_sem.at[j]
                )
                for j in range(col_tiles)
            ]
            for write in writes:
                write.start()
        for side in range(SIDES):
            slot_copy(r, side, 0, slots).wait_recv()

    last = rounds - 1
    for j in range(col_tiles):
        def last_part(i, carry):
            total = arrived(last, i * col_tiles + j)
            mix[i, j] = mix[i, j] + NEIGHBOUR_WEIGHT * total
            cur[i, j] = cur[i, j] + CONSENSUS * NEIGHBOUR_WEIGHT * total
            return carry

        lax.fori_loop(0, row_tiles, last_part, 0)
        for place, (held, target) in enumerate(((cur, params_out), (mix, mixed_out))):
            write = pltpu.make_async_copy(
                held.at[:, j], target.at[:, :, pl.ds(j * TILE, TILE)],
                out_sem.at[(1 + place) * col_tiles + j],
            )
            write.start()
            writes.append(write)
    for r in range(rounds):
        for side in range(SIDES):
            slot_copy(r, side, 0, slots).wait_send()
    for write in writes:
        write.wait()


def solution(mesh):
    sizes = (mesh.shape["wide"], mesh.shape["narrow"])

    def on_device(params, public, mixed, inputs, cotangent, block_ids, block_counts):
        rounds, slots = block_ids.shape[2:]
        rows, cols = params.shape[2:]
        tokens = inputs.shape[2]
        col_tiles = cols // TILE
        banded = (rows // TILE, TILE, cols)
        held = pltpu.VMEM((rows // TILE, col_tiles, TILE, TILE), jnp.float32)
        any_spec = pl.BlockSpec(memory_space=pl.ANY)
        smem_spec = pl.BlockSpec(memory_space=pltpu.SMEM)
        shape = jax.ShapeDtypeStruct(banded, jnp.float32)
        ids = block_ids.reshape(rounds, slots)
        outs = pl.pallas_call(
            functools.partial(kernel, sizes, rounds, slots),
            out_shape=(shape, shape, shape),
            in_specs=[smem_spec] * 4 + [any_spec] * 5,
            out_specs=(any_spec,) * 3,
            scratch_shapes=[
                pltpu.VMEM((tokens, rows), inputs.dtype),
                pltpu.VMEM((tokens, cols), cotangent.dtype),
                held, held, held,
                pltpu.VMEM((1 + SIDES, SUBLANES, TILE), jnp.int32),
                pltpu.SMEM((1 + SIDES, SUBLANES, TILE), jnp.int32),
                pltpu.SemaphoreType.DMA((2 + 3 * col_tiles,)),
                pltpu.SemaphoreType.DMA((SIDES,)),
                pltpu.SemaphoreType.DMA((SIDES,)),
                pltpu.SemaphoreType.DMA,
                pltpu.SemaphoreType.DMA((rounds, SIDES)),
                pltpu.SemaphoreType.DMA((rounds, SIDES)),
                pltpu.SemaphoreType.DMA((3 * col_tiles,)),
            ]
            + [pltpu.VMEM((slots + 1, TILE, TILE), jnp.float32)] * rounds
            + [pltpu.VMEM((SIDES, slots + 1, TILE, TILE), jnp.float32)] * rounds,
            compiler_params=pltpu.CompilerParams(
                collective_id=0, has_side_effects=True, vmem_limit_bytes=48 * 1024 * 1024
            ),
            cost_estimate=pl.CostEstimate(
                flops=2 * tokens * rows * cols, bytes_accessed=6 * 4 * rows * cols, transcendentals=0
            ),
        )(
            ids, ids // col_tiles, ids % col_tiles, block_counts.reshape(rounds),
            params.reshape(banded), public.reshape(banded), mixed.reshape(banded), inputs, cotangent,
        )
        return tuple(out.reshape(params.shape) for out in outs)

    spec = P("wide", "narrow", None, None)
    return jax.shard_map(
        on_device, mesh=mesh, in_specs=(spec,) * 6 + (P("wide", "narrow", None),),
        out_specs=(spec,) * 3, check_vma=False,
    )
```

```python
import functools

import jax
import jax.numpy as jnp
from jax import lax
from jax.experimental import pallas as pl
from jax.experimental.pallas import tpu as pltpu
from jax.sharding import PartitionSpec as P

TILE = 128
LEARN_RATE = 0.05
NEIGHBOUR_WEIGHT = 0.2
CONSENSUS = 0.4
CHUNK = 256
STEP_BANDS = 2
LIMIT = 24 * 1024 * 1024
SUBLANES = 8
SIDES = 4
MESH = pl.DeviceIdType.MESH


def in_hbm(x):
    return pltpu.with_memory_space_constraint(x, pltpu.HBM)


def kernel(
    sizes, rounds, slots, ids_in, counts_in, params, public, mixed, inputs, cotangent,
    cur_out, pub_out, mix_out, maps_out, last_recv,
    ids, counts, acts, cots, cur, pub, mix, places, maps, map_table, load_sem, map_send, map_recv, table_sem,
    send_sem, recv_sem, out_sem, *buffers
):
    sends, recvs = buffers[:rounds], buffers[rounds:] + (last_recv,)
    row_tiles, col_tiles = cur.shape[:2]
    rows = row_tiles * TILE
    wide, narrow = lax.axis_index("wide"), lax.axis_index("narrow")
    wide_size, narrow_size = sizes
    partners = (
        (wide, lax.rem(narrow + 1, narrow_size)),
        (wide, lax.rem(narrow + narrow_size - 1, narrow_size)),
        (lax.rem(wide + 1, wide_size), narrow),
        (lax.rem(wide + wide_size - 1, wide_size), narrow),
    )

    load_lists = [
        pltpu.make_async_copy(ids_in, ids, load_sem.at[2 + 3 * col_tiles]),
        pltpu.make_async_copy(counts_in, counts, load_sem.at[3 + 3 * col_tiles]),
    ]
    load_acts = pltpu.make_async_copy(inputs.at[0, 0], acts, load_sem.at[0])
    load_cots = pltpu.make_async_copy(cotangent.at[0, 0], cots, load_sem.at[1])

    def column_loads(source, held, first):
        return [
            pltpu.make_async_copy(
                source.at[:, :, pl.ds(j * TILE, TILE)], held.at[:, j], load_sem.at[first + j]
            )
            for j in range(col_tiles)
        ]

    load_cur = column_loads(params, cur, 2)
    load_pub = column_loads(public, pub, 2 + col_tiles)
    load_mix = column_loads(mixed, mix, 2 + 2 * col_tiles)
    for load in load_lists + [load_acts, load_cots] + load_cur + load_pub + load_mix:
        load.start()

    barrier = pltpu.get_barrier_semaphore()
    for partner in partners:
        pl.semaphore_signal(barrier, inc=1, device_id=partner, device_id_type=MESH)

    row = lax.broadcasted_iota(jnp.int32, (SUBLANES, TILE), 0)
    lane = lax.broadcasted_iota(jnp.int32, (SUBLANES, TILE), 1)
    for load in load_lists:
        load.wait()
    own_map = jnp.full((SUBLANES, TILE), slots, jnp.int32)
    for r in range(rounds):
        for s in range(slots):
            used = jnp.full((SUBLANES, TILE), counts[0, 0, r], jnp.int32) > s
            own_map = jnp.where((row == r) & (lane == ids[0, 0, r, s]) & used, s, own_map)
    maps[0] = own_map
    for r in range(rounds):
        sends[r][slots] = jnp.zeros((TILE, TILE), jnp.float32)
    for r in range(rounds - 1):
        for side in range(SIDES):
            recvs[r][side, slots] = jnp.zeros((TILE, TILE), jnp.float32)

    for tile in range(row_tiles * col_tiles):
        places[0, tile] = tile // col_tiles
        places[1, tile] = tile % col_tiles

    pl.semaphore_wait(barrier, SIDES)
    map_copies = [
        pltpu.make_async_remote_copy(
            src_ref=maps.at[0], dst_ref=maps.at[1 + side], send_sem=map_send.at[side],
            recv_sem=map_recv.at[side], device_id=partners[side], device_id_type=MESH,
        )
        for side in range(SIDES)
    ]
    for copy in map_copies:
        copy.start()

    def slot_copy(r, side, first, size):
        return pltpu.make_async_remote_copy(
            src_ref=sends[r].at[pl.ds(first, size)],
            dst_ref=recvs[r].at[side, pl.ds(first, size)],
            send_sem=send_sem.at[r, side], recv_sem=recv_sem.at[r, side],
            device_id=partners[side], device_id_type=MESH,
        )

    def arrived(r, tile):
        total = recvs[r][0, map_table[1, r, tile]]
        for side in range(1, SIDES):
            total = total + recvs[r][side, map_table[1 + side, r, tile]]
        return total

    load_acts.wait()
    load_cots.wait()
    for load in load_cur:
        load.wait()
    for first in range(0, rows, CHUNK):
        gradient = lax.dot_general(
            acts[:, first:first + CHUNK], cots[...], (((0,), (0,)), ((), ())),
            preferred_element_type=jnp.float32,
        )
        for j in range(col_tiles):
            for i in range(CHUNK // TILE):
                part = gradient[i * TILE:(i + 1) * TILE, j * TILE:(j + 1) * TILE]
                at = first // TILE + i
                cur[at, j] = cur[at, j] - LEARN_RATE * part
    for load in load_pub:
        load.wait()

    for r in range(rounds):
        for s in range(slots):
            tile = ids[0, 0, r, s]
            i, j = places[0, tile], places[1, tile]
            value = cur[i, j]
            if r:
                value = value + CONSENSUS * NEIGHBOUR_WEIGHT * arrived(r - 1, tile)
            sends[r][s] = value - pub[i, j]
            for side in range(SIDES):
                slot_copy(r, side, s, 1).start()

        if r == 0:
            for copy in map_copies:
                copy.wait()
            table = pltpu.make_async_copy(maps, map_table, table_sem)
            table.start()
            table.wait()
            for load in load_mix:
                load.wait()

        for j in range(col_tiles):
            def own_part(i, carry):
                tile = i * col_tiles + j
                q = sends[r][map_table[0, r, tile]]
                new_pub = pub[i, j] + q
                new_cur, new_mix = cur[i, j], mix[i, j]
                if r:
                    total = arrived(r - 1, tile)
                    new_cur = new_cur + CONSENSUS * NEIGHBOUR_WEIGHT * total
                    q = q + total
                new_mix = new_mix + NEIGHBOUR_WEIGHT * q
                pub[i, j] = new_pub
                mix[i, j] = new_mix
                cur[i, j] = new_cur + CONSENSUS * (new_mix - new_pub)
                return carry

            lax.fori_loop(0, row_tiles, own_part, 0)

        if r == rounds - 1:
            writes = [
                pltpu.make_async_copy(held, target, out_sem.at[n])
                for n, (held, target) in enumerate(
                    ((cur, cur_out), (pub, pub_out), (mix, mix_out), (maps, maps_out))
                )
            ]
            for write in writes:
                write.start()
        for side in range(SIDES):
            slot_copy(r, side, 0, slots).wait_recv()

    for r in range(rounds):
        for side in range(SIDES):
            slot_copy(r, side, 0, slots).wait_send()
    for write in writes:
        write.wait()


def finish(last, table, cur, pub, mix, arrivals, params_out, public_out, mixed_out):
    bands, col_tiles = cur.shape[:2]
    slots = arrivals.shape[1]
    for band in range(bands):
        for j in range(col_tiles):
            tile = (pl.program_id(0) * bands + band) * col_tiles + j
            total = jnp.zeros((TILE, TILE), jnp.float32)
            for side in range(SIDES):
                slot = table[1 + side, last, tile]
                part = arrivals[side, jnp.minimum(slot, slots - 1)]
                total = total + jnp.where(slot < slots, part, 0.0)
            at = (band, slice(None), slice(j * TILE, (j + 1) * TILE))
            params_out[at] = cur[band, j] + CONSENSUS * NEIGHBOUR_WEIGHT * total
            mixed_out[at] = mix[band, j] + NEIGHBOUR_WEIGHT * total
            public_out[at] = pub[band, j]


def solution(mesh):
    sizes = (mesh.shape["wide"], mesh.shape["narrow"])

    def on_device(params, public, mixed, inputs, cotangent, block_ids, block_counts):
        rounds, slots = block_ids.shape[2:]
        rows, cols = params.shape[2:]
        tokens = inputs.shape[2]
        col_tiles = cols // TILE
        banded = (rows // TILE, TILE, cols)
        held = pltpu.VMEM((rows // TILE, col_tiles, TILE, TILE), jnp.float32)
        any_spec = pl.BlockSpec(memory_space=pl.ANY)
        smem_spec = pl.BlockSpec(memory_space=pltpu.SMEM)
        row_tiles = rows // TILE
        tiled = jax.ShapeDtypeStruct((row_tiles, col_tiles, TILE, TILE), jnp.float32)
        maps_shape = (1 + SIDES, SUBLANES, TILE)
        slots_shape = (SIDES, slots, TILE, TILE)
        cur, pub, mix, table, arrivals = pl.pallas_call(
            functools.partial(kernel, sizes, rounds, slots),
            out_shape=(
                tiled, tiled, tiled,
                jax.ShapeDtypeStruct(maps_shape, jnp.int32),
                jax.ShapeDtypeStruct(slots_shape, jnp.float32),
            ),
            in_specs=[any_spec] * 7,
            out_specs=(any_spec,) * 5,
            scratch_shapes=[
                pltpu.SMEM(block_ids.shape, jnp.int32),
                pltpu.SMEM(block_counts.shape, jnp.int32),
                pltpu.VMEM((tokens, rows), inputs.dtype),
                pltpu.VMEM((tokens, cols), cotangent.dtype),
                held, held, held,
                pltpu.SMEM((2, row_tiles * col_tiles), jnp.int32),
                pltpu.VMEM(maps_shape, jnp.int32),
                pltpu.SMEM(maps_shape, jnp.int32),
                pltpu.SemaphoreType.DMA((4 + 3 * col_tiles,)),
                pltpu.SemaphoreType.DMA((SIDES,)),
                pltpu.SemaphoreType.DMA((SIDES,)),
                pltpu.SemaphoreType.DMA,
                pltpu.SemaphoreType.DMA((rounds, SIDES)),
                pltpu.SemaphoreType.DMA((rounds, SIDES)),
                pltpu.SemaphoreType.DMA((4,)),
            ]
            + [pltpu.VMEM((slots + 1, TILE, TILE), jnp.float32)] * rounds
            + [pltpu.VMEM((SIDES, slots + 1, TILE, TILE), jnp.float32)] * (rounds - 1),
            compiler_params=pltpu.CompilerParams(
                collective_id=0, has_side_effects=True, vmem_limit_bytes=LIMIT
            ),
            cost_estimate=pl.CostEstimate(
                flops=2 * tokens * rows * cols, bytes_accessed=6 * 4 * rows * cols, transcendentals=0
            ),
        )(
            in_hbm(block_ids), in_hbm(block_counts),
            *(in_hbm(x.reshape(banded)) for x in (params, public, mixed)),
            in_hbm(inputs), in_hbm(cotangent),
        )
        group = STEP_BANDS
        tiled_spec = pl.BlockSpec((group, col_tiles, TILE, TILE), lambda n: (n, 0, 0, 0))
        out_spec = pl.BlockSpec((group, TILE, cols), lambda n: (n, 0, 0))
        outs = pl.pallas_call(
            functools.partial(finish, rounds - 1),
            grid=(row_tiles // group,),
            out_shape=(jax.ShapeDtypeStruct(banded, jnp.float32),) * 3,
            in_specs=[smem_spec, tiled_spec, tiled_spec, tiled_spec]
            + [pl.BlockSpec(slots_shape, lambda n: (0, 0, 0, 0))],
            out_specs=(out_spec,) * 3,
            compiler_params=pltpu.CompilerParams(vmem_limit_bytes=LIMIT),
            cost_estimate=pl.CostEstimate(
                flops=8 * rows * cols, bytes_accessed=8 * 4 * rows * cols, transcendentals=0
            ),
        )(table, cur, pub, mix, arrivals)
        return tuple(out.reshape(params.shape) for out in outs)

    spec = P("wide", "narrow", None, None)
    return jax.shard_map(
        on_device, mesh=mesh, in_specs=(spec,) * 6 + (P("wide", "narrow", None),),
        out_specs=(spec,) * 3, check_vma=False,
    )
```

```python
import functools

import jax
import jax.numpy as jnp
from jax import lax
from jax.experimental import pallas as pl
from jax.experimental.pallas import tpu as pltpu
from jax.sharding import PartitionSpec as P

TILE = 128
LEARN_RATE = 0.05
NEIGHBOUR_WEIGHT = 0.2
CONSENSUS = 0.4
LIMIT = 24 * 1024 * 1024
SUBLANES = 8
SIDES = 4
MESH = pl.DeviceIdType.MESH


def in_hbm(x):
    return pltpu.with_memory_space_constraint(x, pltpu.HBM)


def in_vmem(x):
    return pltpu.with_memory_space_constraint(x, pltpu.VMEM)


def kernel(
    sizes, rounds, slots, ids_in, counts_in, params, public, mixed, inputs, cotangent,
    cur_out, pub_out, mix_out, maps_out, last_recv,
    ids, counts, acts, cots, cur, pub, mix, places, maps, map_table, load_sem, map_send, map_recv, table_sem,
    send_sem, recv_sem, out_sem, *buffers
):
    sends, recvs = buffers[:rounds], buffers[rounds:] + (last_recv,)
    row_tiles, col_tiles = cur.shape[:2]
    wide, narrow = lax.axis_index("wide"), lax.axis_index("narrow")
    wide_size, narrow_size = sizes
    partners = (
        (wide, lax.rem(narrow + 1, narrow_size)),
        (wide, lax.rem(narrow + narrow_size - 1, narrow_size)),
        (lax.rem(wide + 1, wide_size), narrow),
        (lax.rem(wide + wide_size - 1, wide_size), narrow),
    )

    load_lists = [
        pltpu.make_async_copy(ids_in, ids, load_sem.at[2 + 3 * col_tiles]),
        pltpu.make_async_copy(counts_in, counts, load_sem.at[3 + 3 * col_tiles]),
    ]
    def column_loads(source, held, first):
        return [
            pltpu.make_async_copy(
                source.at[:, :, pl.ds(j * TILE, TILE)], held.at[:, j], load_sem.at[first + j]
            )
            for j in range(col_tiles)
        ]

    def layer_loads(source, held, first):
        return [
            pltpu.make_async_copy(
                source.at[0, 0, :, pl.ds(n * TILE, TILE)], held.at[n], load_sem.at[first + n]
            )
            for n in range(held.shape[0])
        ]

    load_cur = column_loads(params, cur, 0)
    load_pub = column_loads(public, pub, col_tiles)
    load_mix = column_loads(mixed, mix, 2 * col_tiles)
    load_layer = layer_loads(cotangent, cots, 4 + 3 * col_tiles)
    load_layer += layer_loads(inputs, acts, 4 + 4 * col_tiles)
    for load in load_lists + load_layer + load_cur + load_pub:
        load.start()

    barrier = pltpu.get_barrier_semaphore()
    for partner in partners:
        pl.semaphore_signal(barrier, inc=1, device_id=partner, device_id_type=MESH)

    row = lax.broadcasted_iota(jnp.int32, (SUBLANES, TILE), 0)
    lane = lax.broadcasted_iota(jnp.int32, (SUBLANES, TILE), 1)
    for load in load_lists:
        load.wait()
    own_map = jnp.full((SUBLANES, TILE), slots, jnp.int32)
    for r in range(rounds):
        for s in range(slots):
            used = jnp.full((SUBLANES, TILE), counts[0, 0, r], jnp.int32) > s
            own_map = jnp.where((row == r) & (lane == ids[0, 0, r, s]) & used, s, own_map)
    maps[0] = own_map
    for r in range(rounds):
        sends[r][slots] = jnp.zeros((TILE, TILE), jnp.float32)
    for r in range(rounds - 1):
        for side in range(SIDES):
            recvs[r][side, slots] = jnp.zeros((TILE, TILE), jnp.float32)

    for tile in range(row_tiles * col_tiles):
        places[0, tile] = tile // col_tiles
        places[1, tile] = tile % col_tiles

    pl.semaphore_wait(barrier, SIDES)
    map_copies = [
        pltpu.make_async_remote_copy(
            src_ref=maps.at[0], dst_ref=maps.at[1 + side], send_sem=map_send.at[side],
            recv_sem=map_recv.at[side], device_id=partners[side], device_id_type=MESH,
        )
        for side in range(SIDES)
    ]
    for copy in map_copies:
        copy.start()

    def slot_copy(r, side, first, size):
        return pltpu.make_async_remote_copy(
            src_ref=sends[r].at[pl.ds(first, size)],
            dst_ref=recvs[r].at[side, pl.ds(first, size)],
            send_sem=send_sem.at[r, side], recv_sem=recv_sem.at[r, side],
            device_id=partners[side], device_id_type=MESH,
        )

    def arrived(r, tile):
        total = recvs[r][0, map_table[1, r, tile]]
        for side in range(1, SIDES):
            total = total + recvs[r][side, map_table[1 + side, r, tile]]
        return total

    def stepped(i, j):
        gradient = lax.dot_general(
            acts[i], cots[j], (((0,), (0,)), ((), ())), preferred_element_type=jnp.float32
        )
        return cur[i, j] - LEARN_RATE * gradient

    for load in load_layer + load_cur + load_pub:
        load.wait()
    for load in load_mix:
        load.start()

    for r in range(rounds):
        for s in range(slots):
            tile = ids[0, 0, r, s]
            i, j = places[0, tile], places[1, tile]
            if r == 0:
                value = stepped(i, j)
            else:
                value = cur[i, j] + CONSENSUS * NEIGHBOUR_WEIGHT * arrived(r - 1, tile)
            sends[r][s] = value - pub[i, j]
            for side in range(SIDES):
                slot_copy(r, side, s, 1).start()

        if r == 0:
            for copy in map_copies:
                copy.wait()
            table = pltpu.make_async_copy(maps, map_table, table_sem)
            table.start()
            table.wait()
            for load in load_mix:
                load.wait()

            def gradient_step(i, carry):
                for j in range(col_tiles):
                    cur[i, j] = stepped(i, j)
                return carry

            lax.fori_loop(0, row_tiles, gradient_step, 0)

        for j in range(col_tiles):
            def own_part(i, carry):
                tile = i * col_tiles + j
                q = sends[r][map_table[0, r, tile]]
                new_pub = pub[i, j] + q
                new_cur, new_mix = cur[i, j], mix[i, j]
                if r:
                    total = arrived(r - 1, tile)
                    new_cur = new_cur + CONSENSUS * NEIGHBOUR_WEIGHT * total
                    q = q + total
                new_mix = new_mix + NEIGHBOUR_WEIGHT * q
                pub[i, j] = new_pub
                mix[i, j] = new_mix
                cur[i, j] = new_cur + CONSENSUS * (new_mix - new_pub)
                return carry

            lax.fori_loop(0, row_tiles, own_part, 0)

        if r == rounds - 1:
            writes = [
                pltpu.make_async_copy(held, target, out_sem.at[n])
                for n, (held, target) in enumerate(
                    ((cur, cur_out), (pub, pub_out), (mix, mix_out), (maps, maps_out))
                )
            ]
            for write in writes:
                write.start()
        for side in range(SIDES):
            slot_copy(r, side, 0, slots).wait_recv()

    for r in range(rounds):
        for side in range(SIDES):
            slot_copy(r, side, 0, slots).wait_send()
    for write in writes:
        write.wait()


def finish(
    last, table_in, cur, pub, mix, arrivals, params_out, public_out, mixed_out,
    table, new_cur, new_mix, table_sem, pub_sem, out_sem
):
    row_tiles, col_tiles = cur.shape[:2]
    slots = arrivals.shape[1]
    load = pltpu.make_async_copy(table_in, table, table_sem)
    load.start()
    copies = [
        pltpu.make_async_copy(
            pub.at[:, j], public_out.at[:, :, pl.ds(j * TILE, TILE)], pub_sem.at[j]
        )
        for j in range(col_tiles)
    ]
    for copy in copies:
        copy.start()
    load.wait()

    def writes(i):
        return (
            pltpu.make_async_copy(new_cur.at[i], params_out.at[i], out_sem.at[0, i]),
            pltpu.make_async_copy(new_mix.at[i], mixed_out.at[i], out_sem.at[1, i]),
        )

    def one_band(i, carry):
        for j in range(col_tiles):
            total = jnp.zeros((TILE, TILE), jnp.float32)
            for side in range(SIDES):
                slot = table[1 + side, last, i * col_tiles + j]
                part = arrivals[side, jnp.minimum(slot, slots - 1)]
                total = total + jnp.where(slot < slots, part, 0.0)
            span = slice(j * TILE, (j + 1) * TILE)
            new_cur[i, :, span] = cur[i, j] + CONSENSUS * NEIGHBOUR_WEIGHT * total
            new_mix[i, :, span] = mix[i, j] + NEIGHBOUR_WEIGHT * total
        for write in writes(i):
            write.start()
        return carry

    def drain(i, carry):
        for write in writes(i):
            write.wait()
        return carry

    lax.fori_loop(0, row_tiles, one_band, 0)
    lax.fori_loop(0, row_tiles, drain, 0)
    for copy in copies:
        copy.wait()


def solution(mesh):
    sizes = (mesh.shape["wide"], mesh.shape["narrow"])

    def on_device(params, public, mixed, inputs, cotangent, block_ids, block_counts):
        rounds, slots = block_ids.shape[2:]
        rows, cols = params.shape[2:]
        tokens = inputs.shape[2]
        col_tiles = cols // TILE
        banded = (rows // TILE, TILE, cols)
        held = pltpu.VMEM((rows // TILE, col_tiles, TILE, TILE), jnp.float32)
        any_spec = pl.BlockSpec(memory_space=pl.ANY)
        row_tiles = rows // TILE
        tiled = jax.ShapeDtypeStruct((row_tiles, col_tiles, TILE, TILE), jnp.float32)
        maps_shape = (1 + SIDES, SUBLANES, TILE)
        slots_shape = (SIDES, slots, TILE, TILE)
        cur, pub, mix, table, arrivals = pl.pallas_call(
            functools.partial(kernel, sizes, rounds, slots),
            out_shape=(
                tiled, tiled, tiled,
                jax.ShapeDtypeStruct(maps_shape, jnp.int32),
                jax.ShapeDtypeStruct(slots_shape, jnp.float32),
            ),
            in_specs=[any_spec] * 7,
            out_specs=(any_spec,) * 5,
            scratch_shapes=[
                pltpu.SMEM(block_ids.shape, jnp.int32),
                pltpu.SMEM(block_counts.shape, jnp.int32),
                pltpu.VMEM((row_tiles, tokens, TILE), inputs.dtype),
                pltpu.VMEM((col_tiles, tokens, TILE), cotangent.dtype),
                held, held, held,
                pltpu.SMEM((2, row_tiles * col_tiles), jnp.int32),
                pltpu.VMEM(maps_shape, jnp.int32),
                pltpu.SMEM(maps_shape, jnp.int32),
                pltpu.SemaphoreType.DMA((4 + 4 * col_tiles + row_tiles,)),
                pltpu.SemaphoreType.DMA((SIDES,)),
                pltpu.SemaphoreType.DMA((SIDES,)),
                pltpu.SemaphoreType.DMA,
                pltpu.SemaphoreType.DMA((rounds, SIDES)),
                pltpu.SemaphoreType.DMA((rounds, SIDES)),
                pltpu.SemaphoreType.DMA((4,)),
            ]
            + [pltpu.VMEM((slots + 1, TILE, TILE), jnp.float32)] * rounds
            + [pltpu.VMEM((SIDES, slots + 1, TILE, TILE), jnp.float32)] * (rounds - 1),
            compiler_params=pltpu.CompilerParams(
                collective_id=0, has_side_effects=True, vmem_limit_bytes=LIMIT
            ),
            cost_estimate=pl.CostEstimate(
                flops=2 * tokens * rows * cols, bytes_accessed=6 * 4 * rows * cols, transcendentals=0
            ),
        )(
            in_hbm(block_ids), in_hbm(block_counts),
            *(in_hbm(x.reshape(banded)) for x in (params, public, mixed)),
            in_hbm(inputs), in_hbm(cotangent),
        )
        vmem_spec = pl.BlockSpec(memory_space=pltpu.VMEM)
        outs = pl.pallas_call(
            functools.partial(finish, rounds - 1),
            out_shape=(jax.ShapeDtypeStruct(banded, jnp.float32),) * 3,
            in_specs=[any_spec, vmem_spec, any_spec, vmem_spec, vmem_spec],
            out_specs=(any_spec,) * 3,
            scratch_shapes=[
                pltpu.SMEM(maps_shape, jnp.int32),
                pltpu.VMEM(banded, jnp.float32),
                pltpu.VMEM(banded, jnp.float32),
                pltpu.SemaphoreType.DMA,
                pltpu.SemaphoreType.DMA((col_tiles,)),
                pltpu.SemaphoreType.DMA((2, row_tiles)),
            ],
            compiler_params=pltpu.CompilerParams(vmem_limit_bytes=LIMIT),
            cost_estimate=pl.CostEstimate(
                flops=8 * rows * cols, bytes_accessed=8 * 4 * rows * cols, transcendentals=0
            ),
        )(table, in_vmem(cur), pub, in_vmem(mix), in_vmem(arrivals))
        return tuple(out.reshape(params.shape) for out in outs)

    spec = P("wide", "narrow", None, None)
    return jax.shard_map(
        on_device, mesh=mesh, in_specs=(spec,) * 6 + (P("wide", "narrow", None),),
        out_specs=(spec,) * 3, check_vma=False,
    )
```

```python
import functools

import jax
import jax.numpy as jnp
from jax import lax
from jax.experimental import pallas as pl
from jax.experimental.pallas import tpu as pltpu
from jax.sharding import PartitionSpec as P

TILE = 128
LEARN_RATE = 0.05
NEIGHBOUR_WEIGHT = 0.2
CONSENSUS = 0.4
LIMIT = 24 * 1024 * 1024
SUBLANES = 8
SIDES = 4
NEAR = 2
MESH = pl.DeviceIdType.MESH


def in_hbm(x):
    return pltpu.with_memory_space_constraint(x, pltpu.HBM)


def in_vmem(x):
    return pltpu.with_memory_space_constraint(x, pltpu.VMEM)


def kernel(
    sizes, rounds, slots, ids_in, counts_in, params, public, mixed, inputs, cotangent,
    cur_out, pub_out, mix_out, maps_out, last_recv,
    ids, counts, acts, cots, cur, pub, mix, places, maps, map_table, load_sem, map_send, map_recv, table_sem,
    send_sem, recv_sem, out_sem, *buffers
):
    sends, wide_recvs = buffers[:rounds], buffers[rounds:2 * rounds]
    narrow_recvs = buffers[2 * rounds:] + (last_recv,)
    row_tiles, col_tiles = cur.shape[:2]
    wide, narrow = lax.axis_index("wide"), lax.axis_index("narrow")
    wide_size, narrow_size = sizes
    partners = (
        (wide, lax.rem(narrow + 1, narrow_size)),
        (wide, lax.rem(narrow + narrow_size - 1, narrow_size)),
        (lax.rem(wide + 1, wide_size), narrow),
        (lax.rem(wide + wide_size - 1, wide_size), narrow),
    )

    barrier = pltpu.get_barrier_semaphore()
    for partner in partners:
        pl.semaphore_signal(barrier, inc=1, device_id=partner, device_id_type=MESH)

    load_lists = [
        pltpu.make_async_copy(ids_in, ids, load_sem.at[2 + 3 * col_tiles]),
        pltpu.make_async_copy(counts_in, counts, load_sem.at[3 + 3 * col_tiles]),
    ]
    def column_loads(source, held, first):
        return [
            pltpu.make_async_copy(
                source.at[:, :, pl.ds(j * TILE, TILE)], held.at[:, j], load_sem.at[first + j]
            )
            for j in range(col_tiles)
        ]

    def layer_loads(source, held, first):
        return [
            pltpu.make_async_copy(
                source.at[0, 0, :, pl.ds(n * TILE, TILE)], held.at[n], load_sem.at[first + n]
            )
            for n in range(held.shape[0])
        ]

    load_cur = column_loads(params, cur, 0)
    load_pub = column_loads(public, pub, col_tiles)
    load_mix = column_loads(mixed, mix, 2 * col_tiles)
    load_layer = layer_loads(cotangent, cots, 4 + 3 * col_tiles)
    load_layer += layer_loads(inputs, acts, 4 + 4 * col_tiles)
    for load in load_lists + load_layer + load_cur + load_pub:
        load.start()

    row = lax.broadcasted_iota(jnp.int32, (SUBLANES, TILE), 0)
    lane = lax.broadcasted_iota(jnp.int32, (SUBLANES, TILE), 1)
    for load in load_lists:
        load.wait()
    own_map = jnp.full((SUBLANES, TILE), slots, jnp.int32)
    for r in range(rounds):
        for s in range(slots):
            used = jnp.full((SUBLANES, TILE), counts[0, 0, r], jnp.int32) > s
            own_map = jnp.where((row == r) & (lane == ids[0, 0, r, s]) & used, s, own_map)
    maps[0] = own_map
    for r in range(rounds):
        sends[r][slots] = jnp.zeros((TILE, TILE), jnp.float32)
    for held in wide_recvs + narrow_recvs[:-1]:
        for side in range(NEAR):
            held[side, slots] = jnp.zeros((TILE, TILE), jnp.float32)

    for tile in range(row_tiles * col_tiles):
        places[0, tile] = tile // col_tiles
        places[1, tile] = tile % col_tiles

    pl.semaphore_wait(barrier, SIDES)
    map_copies = [
        pltpu.make_async_remote_copy(
            src_ref=maps.at[0], dst_ref=maps.at[1 + side], send_sem=map_send.at[side],
            recv_sem=map_recv.at[side], device_id=partners[side], device_id_type=MESH,
        )
        for side in range(SIDES)
    ]
    for copy in map_copies:
        copy.start()

    def slot_copy(r, side, first, size):
        recvs = narrow_recvs if side < NEAR else wide_recvs
        return pltpu.make_async_remote_copy(
            src_ref=sends[r].at[pl.ds(first, size)],
            dst_ref=recvs[r].at[side % NEAR, pl.ds(first, size)],
            send_sem=send_sem.at[r, side], recv_sem=recv_sem.at[r, side],
            device_id=partners[side], device_id_type=MESH,
        )

    def arrived(held, first_side, r, tile):
        total = held[r][0, map_table[1 + first_side, r, tile]]
        for side in range(1, NEAR):
            total = total + held[r][side, map_table[1 + first_side + side, r, tile]]
        return total

    def gradient(i, j):
        return lax.dot_general(
            acts[i], cots[j], (((0,), (0,)), ((), ())), preferred_element_type=jnp.float32
        )

    def place(r, s):
        tile = ids[0, 0, r, s]
        return tile, places[0, tile], places[1, tile]

    for load in load_layer:
        load.wait()
    for s in range(slots):
        _, i, j = place(0, s)
        sends[0][s] = LEARN_RATE * gradient(i, j)
    for load in load_cur + load_pub:
        load.wait()
    for load in load_mix:
        load.start()

    for r in range(rounds):
        for s in range(slots):
            tile, i, j = place(r, s)
            if r == 0:
                value = cur[i, j] - sends[r][s]
            else:
                value = cur[i, j] + CONSENSUS * NEIGHBOUR_WEIGHT * arrived(narrow_recvs, 0, r - 1, tile)
            sends[r][s] = value - pub[i, j]
            for side in range(SIDES):
                slot_copy(r, side, s, 1).start()

        if r == 0:
            for copy in map_copies:
                copy.wait()
            table = pltpu.make_async_copy(maps, map_table, table_sem)
            table.start()
            table.wait()
            for load in load_mix:
                load.wait()

            def gradient_step(i, carry):
                for j in range(col_tiles):
                    cur[i, j] = cur[i, j] - LEARN_RATE * gradient(i, j)
                return carry

            lax.fori_loop(0, row_tiles, gradient_step, 0)

        for j in range(col_tiles):
            def own_part(i, carry):
                tile = i * col_tiles + j
                q = sends[r][map_table[0, r, tile]]
                new_pub = pub[i, j] + q
                new_cur, new_mix = cur[i, j], mix[i, j]
                if r:
                    total = arrived(narrow_recvs, 0, r - 1, tile)
                    new_cur = new_cur + CONSENSUS * NEIGHBOUR_WEIGHT * total
                    q = q + total
                new_mix = new_mix + NEIGHBOUR_WEIGHT * q
                pub[i, j] = new_pub
                mix[i, j] = new_mix
                cur[i, j] = new_cur + CONSENSUS * (new_mix - new_pub)
                return carry

            lax.fori_loop(0, row_tiles, own_part, 0)

        for side in range(NEAR, SIDES):
            slot_copy(r, side, 0, slots).wait_recv()

        def wide_part(i, carry):
            for j in range(col_tiles):
                total = arrived(wide_recvs, NEAR, r, i * col_tiles + j)
                mix[i, j] = mix[i, j] + NEIGHBOUR_WEIGHT * total
                cur[i, j] = cur[i, j] + CONSENSUS * NEIGHBOUR_WEIGHT * total
            return carry

        lax.fori_loop(0, row_tiles, wide_part, 0)

        if r == rounds - 1:
            writes = [
                pltpu.make_async_copy(held, target, out_sem.at[n])
                for n, (held, target) in enumerate(
                    ((cur, cur_out), (pub, pub_out), (mix, mix_out), (maps, maps_out))
                )
            ]
            for write in writes:
                write.start()
        for side in range(NEAR):
            slot_copy(r, side, 0, slots).wait_recv()

    for r in range(rounds):
        for side in range(SIDES):
            slot_copy(r, side, 0, slots).wait_send()
    for write in writes:
        write.wait()


def finish(
    last, table_in, cur, pub, mix, arrivals, params_out, public_out, mixed_out,
    table, new_cur, new_mix, table_sem, pub_sem, out_sem
):
    row_tiles, col_tiles = cur.shape[:2]
    slots = arrivals.shape[1]
    load = pltpu.make_async_copy(table_in, table, table_sem)
    load.start()
    copies = [
        pltpu.make_async_copy(
            pub.at[:, j], public_out.at[:, :, pl.ds(j * TILE, TILE)], pub_sem.at[j]
        )
        for j in range(col_tiles)
    ]
    for copy in copies:
        copy.start()
    load.wait()

    def writes(i):
        return (
            pltpu.make_async_copy(new_cur.at[i], params_out.at[i], out_sem.at[0, i]),
            pltpu.make_async_copy(new_mix.at[i], mixed_out.at[i], out_sem.at[1, i]),
        )

    def one_band(i, carry):
        for j in range(col_tiles):
            total = jnp.zeros((TILE, TILE), jnp.float32)
            for side in range(NEAR):
                slot = table[1 + side, last, i * col_tiles + j]
                part = arrivals[side, jnp.minimum(slot, slots - 1)]
                total = total + jnp.where(slot < slots, part, 0.0)
            span = slice(j * TILE, (j + 1) * TILE)
            new_cur[i, :, span] = cur[i, j] + CONSENSUS * NEIGHBOUR_WEIGHT * total
            new_mix[i, :, span] = mix[i, j] + NEIGHBOUR_WEIGHT * total
        for write in writes(i):
            write.start()
        return carry

    def drain(i, carry):
        for write in writes(i):
            write.wait()
        return carry

    lax.fori_loop(0, row_tiles, one_band, 0)
    lax.fori_loop(0, row_tiles, drain, 0)
    for copy in copies:
        copy.wait()


def solution(mesh):
    sizes = (mesh.shape["wide"], mesh.shape["narrow"])

    def on_device(params, public, mixed, inputs, cotangent, block_ids, block_counts):
        rounds, slots = block_ids.shape[2:]
        rows, cols = params.shape[2:]
        tokens = inputs.shape[2]
        col_tiles = cols // TILE
        banded = (rows // TILE, TILE, cols)
        held = pltpu.VMEM((rows // TILE, col_tiles, TILE, TILE), jnp.float32)
        any_spec = pl.BlockSpec(memory_space=pl.ANY)
        row_tiles = rows // TILE
        tiled = jax.ShapeDtypeStruct((row_tiles, col_tiles, TILE, TILE), jnp.float32)
        maps_shape = (1 + SIDES, SUBLANES, TILE)
        slots_shape = (NEAR, slots, TILE, TILE)
        cur, pub, mix, table, arrivals = pl.pallas_call(
            functools.partial(kernel, sizes, rounds, slots),
            out_shape=(
                tiled, tiled, tiled,
                jax.ShapeDtypeStruct(maps_shape, jnp.int32),
                jax.ShapeDtypeStruct(slots_shape, jnp.float32),
            ),
            in_specs=[any_spec] * 7,
            out_specs=(any_spec,) * 5,
            scratch_shapes=[
                pltpu.SMEM(block_ids.shape, jnp.int32),
                pltpu.SMEM(block_counts.shape, jnp.int32),
                pltpu.VMEM((row_tiles, tokens, TILE), inputs.dtype),
                pltpu.VMEM((col_tiles, tokens, TILE), cotangent.dtype),
                held, held, held,
                pltpu.SMEM((2, row_tiles * col_tiles), jnp.int32),
                pltpu.VMEM(maps_shape, jnp.int32),
                pltpu.SMEM(maps_shape, jnp.int32),
                pltpu.SemaphoreType.DMA((4 + 4 * col_tiles + row_tiles,)),
                pltpu.SemaphoreType.DMA((SIDES,)),
                pltpu.SemaphoreType.DMA((SIDES,)),
                pltpu.SemaphoreType.DMA,
                pltpu.SemaphoreType.DMA((rounds, SIDES)),
                pltpu.SemaphoreType.DMA((rounds, SIDES)),
                pltpu.SemaphoreType.DMA((4,)),
            ]
            + [pltpu.VMEM((slots + 1, TILE, TILE), jnp.float32)] * rounds
            + [pltpu.VMEM((NEAR, slots + 1, TILE, TILE), jnp.float32)] * (2 * rounds - 1),
            compiler_params=pltpu.CompilerParams(
                collective_id=0, has_side_effects=True, vmem_limit_bytes=LIMIT
            ),
            cost_estimate=pl.CostEstimate(
                flops=2 * tokens * rows * cols, bytes_accessed=6 * 4 * rows * cols, transcendentals=0
            ),
        )(
            in_hbm(block_ids), in_hbm(block_counts),
            *(in_hbm(x.reshape(banded)) for x in (params, public, mixed)),
            in_hbm(inputs), in_hbm(cotangent),
        )
        vmem_spec = pl.BlockSpec(memory_space=pltpu.VMEM)
        outs = pl.pallas_call(
            functools.partial(finish, rounds - 1),
            out_shape=(jax.ShapeDtypeStruct(banded, jnp.float32),) * 3,
            in_specs=[any_spec, vmem_spec, any_spec, vmem_spec, vmem_spec],
            out_specs=(any_spec,) * 3,
            scratch_shapes=[
                pltpu.SMEM(maps_shape, jnp.int32),
                pltpu.VMEM(banded, jnp.float32),
                pltpu.VMEM(banded, jnp.float32),
                pltpu.SemaphoreType.DMA,
                pltpu.SemaphoreType.DMA((col_tiles,)),
                pltpu.SemaphoreType.DMA((2, row_tiles)),
            ],
            compiler_params=pltpu.CompilerParams(vmem_limit_bytes=LIMIT),
            cost_estimate=pl.CostEstimate(
                flops=8 * rows * cols, bytes_accessed=8 * 4 * rows * cols, transcendentals=0
            ),
        )(table, in_vmem(cur), pub, in_vmem(mix), in_vmem(arrivals))
        return tuple(out.reshape(params.shape) for out in outs)

    spec = P("wide", "narrow", None, None)
    return jax.shard_map(
        on_device, mesh=mesh, in_specs=(spec,) * 6 + (P("wide", "narrow", None),),
        out_specs=(spec,) * 3, check_vma=False,
    )
```

```python
import functools

import jax
import jax.numpy as jnp
from jax import lax
from jax.experimental import pallas as pl
from jax.experimental.pallas import tpu as pltpu
from jax.sharding import PartitionSpec as P

TILE = 128
LEARN_RATE = 0.05
NEIGHBOUR_WEIGHT = 0.2
CONSENSUS = 0.4
LIMIT = 24 * 1024 * 1024
SUBLANES = 8
SIDES = 4
NEAR = 2
MESH = pl.DeviceIdType.MESH


def in_hbm(x):
    return pltpu.with_memory_space_constraint(x, pltpu.HBM)


def in_vmem(x):
    return pltpu.with_memory_space_constraint(x, pltpu.VMEM)


def kernel(
    sizes, rounds, slots, ids_in, counts_in, params, public, mixed, inputs, cotangent,
    cur_out, pub_out, mix_out, maps_out, last_recv,
    ids, counts, acts, cots, cur, pub, mix, places, maps, map_table, load_sem, map_send, map_recv, table_sem,
    send_sem, recv_sem, out_sem, *buffers
):
    sends, wide_recvs = buffers[:rounds], buffers[rounds:2 * rounds]
    narrow_recvs = buffers[2 * rounds:] + (last_recv,)
    row_tiles, col_tiles = cur.shape[:2]
    wide, narrow = lax.axis_index("wide"), lax.axis_index("narrow")
    wide_size, narrow_size = sizes
    partners = (
        (wide, lax.rem(narrow + 1, narrow_size)),
        (wide, lax.rem(narrow + narrow_size - 1, narrow_size)),
        (lax.rem(wide + 1, wide_size), narrow),
        (lax.rem(wide + wide_size - 1, wide_size), narrow),
    )

    barrier = pltpu.get_barrier_semaphore()
    for partner in partners:
        pl.semaphore_signal(barrier, inc=1, device_id=partner, device_id_type=MESH)

    load_lists = [
        pltpu.make_async_copy(ids_in, ids, load_sem.at[2 + 3 * col_tiles]),
        pltpu.make_async_copy(counts_in, counts, load_sem.at[3 + 3 * col_tiles]),
    ]
    def column_loads(source, held, first):
        return [
            pltpu.make_async_copy(
                source.at[:, :, pl.ds(j * TILE, TILE)], held.at[:, j], load_sem.at[first + j]
            )
            for j in range(col_tiles)
        ]

    def layer_loads(source, held, first):
        return [
            pltpu.make_async_copy(
                source.at[0, 0, :, pl.ds(n * TILE, TILE)], held.at[n], load_sem.at[first + n]
            )
            for n in range(held.shape[0])
        ]

    load_cur = column_loads(params, cur, 0)
    load_pub = column_loads(public, pub, col_tiles)
    load_mix = column_loads(mixed, mix, 2 * col_tiles)
    load_layer = layer_loads(cotangent, cots, 4 + 3 * col_tiles)
    load_layer += layer_loads(inputs, acts, 4 + 4 * col_tiles)
    for load in load_lists + load_layer + load_cur + load_pub:
        load.start()

    row = lax.broadcasted_iota(jnp.int32, (SUBLANES, TILE), 0)
    lane = lax.broadcasted_iota(jnp.int32, (SUBLANES, TILE), 1)
    for load in load_lists:
        load.wait()
    own_map = jnp.full((SUBLANES, TILE), slots, jnp.int32)
    for r in range(rounds):
        for s in range(slots):
            used = jnp.full((SUBLANES, TILE), counts[0, 0, r], jnp.int32) > s
            own_map = jnp.where((row == r) & (lane == ids[0, 0, r, s]) & used, s, own_map)
    maps[0] = own_map
    for r in range(rounds):
        sends[r][slots] = jnp.zeros((TILE, TILE), jnp.float32)
    for held in wide_recvs + narrow_recvs[:-1]:
        for side in range(NEAR):
            held[side, slots] = jnp.zeros((TILE, TILE), jnp.float32)

    for tile in range(row_tiles * col_tiles):
        places[0, tile] = tile // col_tiles
        places[1, tile] = tile % col_tiles

    pl.semaphore_wait(barrier, SIDES)
    map_copies = [
        pltpu.make_async_remote_copy(
            src_ref=maps.at[0], dst_ref=maps.at[1 + side], send_sem=map_send.at[side],
            recv_sem=map_recv.at[side], device_id=partners[side], device_id_type=MESH,
        )
        for side in range(SIDES)
    ]
    for copy in map_copies:
        copy.start()

    def slot_copy(r, side, first, size):
        recvs = narrow_recvs if side < NEAR else wide_recvs
        return pltpu.make_async_remote_copy(
            src_ref=sends[r].at[pl.ds(first, size)],
            dst_ref=recvs[r].at[side % NEAR, pl.ds(first, size)],
            send_sem=send_sem.at[r, side], recv_sem=recv_sem.at[r, side],
            device_id=partners[side], device_id_type=MESH,
        )

    def arrived(held, first_side, r, tile):
        total = held[r][0, map_table[1 + first_side, r, tile]]
        for side in range(1, NEAR):
            total = total + held[r][side, map_table[1 + first_side + side, r, tile]]
        return total

    def gradient(i, j):
        return lax.dot_general(
            acts[i], cots[j], (((0,), (0,)), ((), ())), preferred_element_type=jnp.float32
        )

    def place(r, s):
        tile = ids[0, 0, r, s]
        return tile, places[0, tile], places[1, tile]

    for load in load_layer:
        load.wait()
    for s in range(slots):
        _, i, j = place(0, s)
        sends[0][s] = LEARN_RATE * gradient(i, j)
    for load in load_cur + load_pub:
        load.wait()
    for load in load_mix:
        load.start()

    for r in range(rounds):
        for s in range(slots):
            tile, i, j = place(r, s)
            if r == 0:
                value = cur[i, j] - sends[r][s]
            else:
                value = cur[i, j] + CONSENSUS * NEIGHBOUR_WEIGHT * arrived(narrow_recvs, 0, r - 1, tile)
            sends[r][s] = value - pub[i, j]
            for side in range(NEAR):
                slot_copy(r, side, s, 1).start()
        for side in range(NEAR, SIDES):
            slot_copy(r, side, 0, slots).start()

        if r == 0:
            for copy in map_copies:
                copy.wait()
            table = pltpu.make_async_copy(maps, map_table, table_sem)
            table.start()
            table.wait()
            for load in load_mix:
                load.wait()

            def gradient_step(i, carry):
                for j in range(col_tiles):
                    cur[i, j] = cur[i, j] - LEARN_RATE * gradient(i, j)
                return carry

            lax.fori_loop(0, row_tiles, gradient_step, 0)

        for j in range(col_tiles):
            def own_part(i, carry):
                tile = i * col_tiles + j
                q = sends[r][map_table[0, r, tile]]
                new_pub = pub[i, j] + q
                new_cur, new_mix = cur[i, j], mix[i, j]
                if r:
                    total = arrived(narrow_recvs, 0, r - 1, tile)
                    new_cur = new_cur + CONSENSUS * NEIGHBOUR_WEIGHT * total
                    q = q + total
                new_mix = new_mix + NEIGHBOUR_WEIGHT * q
                pub[i, j] = new_pub
                mix[i, j] = new_mix
                cur[i, j] = new_cur + CONSENSUS * (new_mix - new_pub)
                return carry

            lax.fori_loop(0, row_tiles, own_part, 0)

        for side in range(NEAR, SIDES):
            slot_copy(r, side, 0, slots).wait_recv()

        def wide_part(i, carry):
            for j in range(col_tiles):
                total = arrived(wide_recvs, NEAR, r, i * col_tiles + j)
                mix[i, j] = mix[i, j] + NEIGHBOUR_WEIGHT * total
                cur[i, j] = cur[i, j] + CONSENSUS * NEIGHBOUR_WEIGHT * total
            return carry

        lax.fori_loop(0, row_tiles, wide_part, 0)

        if r == rounds - 1:
            writes = [
                pltpu.make_async_copy(held, target, out_sem.at[n])
                for n, (held, target) in enumerate(
                    ((cur, cur_out), (pub, pub_out), (mix, mix_out), (maps, maps_out))
                )
            ]
            for write in writes:
                write.start()
        for side in range(NEAR):
            slot_copy(r, side, 0, slots).wait_recv()

    for r in range(rounds):
        for side in range(SIDES):
            slot_copy(r, side, 0, slots).wait_send()
    for write in writes:
        write.wait()


def finish(
    last, table_in, cur, pub, mix, arrivals, params_out, public_out, mixed_out,
    table, new_cur, new_mix, table_sem, pub_sem, out_sem
):
    row_tiles, col_tiles = cur.shape[:2]
    slots = arrivals.shape[1]
    load = pltpu.make_async_copy(table_in, table, table_sem)
    load.start()
    copies = [
        pltpu.make_async_copy(
            pub.at[:, j], public_out.at[:, :, pl.ds(j * TILE, TILE)], pub_sem.at[j]
        )
        for j in range(col_tiles)
    ]
    for copy in copies:
        copy.start()
    load.wait()

    def writes(i):
        return (
            pltpu.make_async_copy(new_cur.at[i], params_out.at[i], out_sem.at[0, i]),
            pltpu.make_async_copy(new_mix.at[i], mixed_out.at[i], out_sem.at[1, i]),
        )

    def one_band(i, carry):
        for j in range(col_tiles):
            total = jnp.zeros((TILE, TILE), jnp.float32)
            for side in range(NEAR):
                slot = table[1 + side, last, i * col_tiles + j]
                part = arrivals[side, jnp.minimum(slot, slots - 1)]
                total = total + jnp.where(slot < slots, part, 0.0)
            span = slice(j * TILE, (j + 1) * TILE)
            new_cur[i, :, span] = cur[i, j] + CONSENSUS * NEIGHBOUR_WEIGHT * total
            new_mix[i, :, span] = mix[i, j] + NEIGHBOUR_WEIGHT * total
        for write in writes(i):
            write.start()
        return carry

    def drain(i, carry):
        for write in writes(i):
            write.wait()
        return carry

    lax.fori_loop(0, row_tiles, one_band, 0)
    lax.fori_loop(0, row_tiles, drain, 0)
    for copy in copies:
        copy.wait()


def solution(mesh):
    sizes = (mesh.shape["wide"], mesh.shape["narrow"])

    def on_device(params, public, mixed, inputs, cotangent, block_ids, block_counts):
        rounds, slots = block_ids.shape[2:]
        rows, cols = params.shape[2:]
        tokens = inputs.shape[2]
        col_tiles = cols // TILE
        banded = (rows // TILE, TILE, cols)
        held = pltpu.VMEM((rows // TILE, col_tiles, TILE, TILE), jnp.float32)
        any_spec = pl.BlockSpec(memory_space=pl.ANY)
        row_tiles = rows // TILE
        tiled = jax.ShapeDtypeStruct((row_tiles, col_tiles, TILE, TILE), jnp.float32)
        maps_shape = (1 + SIDES, SUBLANES, TILE)
        slots_shape = (NEAR, slots, TILE, TILE)
        cur, pub, mix, table, arrivals = pl.pallas_call(
            functools.partial(kernel, sizes, rounds, slots),
            out_shape=(
                tiled, tiled, tiled,
                jax.ShapeDtypeStruct(maps_shape, jnp.int32),
                jax.ShapeDtypeStruct(slots_shape, jnp.float32),
            ),
            in_specs=[any_spec] * 7,
            out_specs=(any_spec,) * 5,
            scratch_shapes=[
                pltpu.SMEM(block_ids.shape, jnp.int32),
                pltpu.SMEM(block_counts.shape, jnp.int32),
                pltpu.VMEM((row_tiles, tokens, TILE), inputs.dtype),
                pltpu.VMEM((col_tiles, tokens, TILE), cotangent.dtype),
                held, held, held,
                pltpu.SMEM((2, row_tiles * col_tiles), jnp.int32),
                pltpu.VMEM(maps_shape, jnp.int32),
                pltpu.SMEM(maps_shape, jnp.int32),
                pltpu.SemaphoreType.DMA((4 + 4 * col_tiles + row_tiles,)),
                pltpu.SemaphoreType.DMA((SIDES,)),
                pltpu.SemaphoreType.DMA((SIDES,)),
                pltpu.SemaphoreType.DMA,
                pltpu.SemaphoreType.DMA((rounds, SIDES)),
                pltpu.SemaphoreType.DMA((rounds, SIDES)),
                pltpu.SemaphoreType.DMA((4,)),
            ]
            + [pltpu.VMEM((slots + 1, TILE, TILE), jnp.float32)] * rounds
            + [pltpu.VMEM((NEAR, slots + 1, TILE, TILE), jnp.float32)] * (2 * rounds - 1),
            compiler_params=pltpu.CompilerParams(
                collective_id=0, has_side_effects=True, vmem_limit_bytes=LIMIT
            ),
            cost_estimate=pl.CostEstimate(
                flops=2 * tokens * rows * cols, bytes_accessed=6 * 4 * rows * cols, transcendentals=0
            ),
        )(
            in_hbm(block_ids), in_hbm(block_counts),
            *(in_hbm(x.reshape(banded)) for x in (params, public, mixed)),
            in_hbm(inputs), in_hbm(cotangent),
        )
        vmem_spec = pl.BlockSpec(memory_space=pltpu.VMEM)
        outs = pl.pallas_call(
            functools.partial(finish, rounds - 1),
            out_shape=(jax.ShapeDtypeStruct(banded, jnp.float32),) * 3,
            in_specs=[any_spec, vmem_spec, any_spec, vmem_spec, vmem_spec],
            out_specs=(any_spec,) * 3,
            scratch_shapes=[
                pltpu.SMEM(maps_shape, jnp.int32),
                pltpu.VMEM(banded, jnp.float32),
                pltpu.VMEM(banded, jnp.float32),
                pltpu.SemaphoreType.DMA,
                pltpu.SemaphoreType.DMA((col_tiles,)),
                pltpu.SemaphoreType.DMA((2, row_tiles)),
            ],
            compiler_params=pltpu.CompilerParams(vmem_limit_bytes=LIMIT),
            cost_estimate=pl.CostEstimate(
                flops=8 * rows * cols, bytes_accessed=8 * 4 * rows * cols, transcendentals=0
            ),
        )(table, in_vmem(cur), pub, in_vmem(mix), in_vmem(arrivals))
        return tuple(out.reshape(params.shape) for out in outs)

    spec = P("wide", "narrow", None, None)
    return jax.shard_map(
        on_device, mesh=mesh, in_specs=(spec,) * 6 + (P("wide", "narrow", None),),
        out_specs=(spec,) * 3, check_vma=False,
    )
```

```python
import functools

import jax
import jax.numpy as jnp
from jax import lax
from jax.experimental import pallas as pl
from jax.experimental.pallas import tpu as pltpu
from jax.sharding import PartitionSpec as P

TILE = 128
LEARN_RATE = 0.05
NEIGHBOUR_WEIGHT = 0.2
CONSENSUS = 0.4
LIMIT = 24 * 1024 * 1024
SUBLANES = 8
SIDES = 4
NEAR = 2
MESH = pl.DeviceIdType.MESH


def in_hbm(x):
    return pltpu.with_memory_space_constraint(x, pltpu.HBM)


def in_vmem(x):
    return pltpu.with_memory_space_constraint(x, pltpu.VMEM)


def kernel(
    sizes, rounds, slots, ids_in, counts_in, params, public, mixed, inputs, cotangent,
    cur_out, pub_out, mix_out, maps_out, last_recv,
    ids, counts, acts, cots, cur, pub, mix, places, maps, map_table, load_sem, map_send, map_recv, table_sem,
    send_sem, recv_sem, out_sem, *buffers
):
    sends, wide_recvs = buffers[:rounds], buffers[rounds:2 * rounds]
    narrow_recvs = buffers[2 * rounds:] + (last_recv,)
    row_tiles, col_tiles = cur.shape[:2]
    wide, narrow = lax.axis_index("wide"), lax.axis_index("narrow")
    wide_size, narrow_size = sizes
    partners = (
        (wide, lax.rem(narrow + 1, narrow_size)),
        (wide, lax.rem(narrow + narrow_size - 1, narrow_size)),
        (lax.rem(wide + 1, wide_size), narrow),
        (lax.rem(wide + wide_size - 1, wide_size), narrow),
    )

    barrier = pltpu.get_barrier_semaphore()
    for partner in partners:
        pl.semaphore_signal(barrier, inc=1, device_id=partner, device_id_type=MESH)

    load_lists = [
        pltpu.make_async_copy(ids_in, ids, load_sem.at[2 + 3 * col_tiles]),
        pltpu.make_async_copy(counts_in, counts, load_sem.at[3 + 3 * col_tiles]),
    ]
    def column_loads(source, held, first):
        return [
            pltpu.make_async_copy(
                source.at[:, :, pl.ds(j * TILE, TILE)], held.at[:, j], load_sem.at[first + j]
            )
            for j in range(col_tiles)
        ]

    def layer_loads(source, held, first):
        return [
            pltpu.make_async_copy(
                source.at[0, 0, :, pl.ds(n * TILE, TILE)], held.at[n], load_sem.at[first + n]
            )
            for n in range(held.shape[0])
        ]

    load_cur = column_loads(params, cur, 0)
    load_pub = column_loads(public, pub, col_tiles)
    load_mix = column_loads(mixed, mix, 2 * col_tiles)
    load_layer = layer_loads(cotangent, cots, 4 + 3 * col_tiles)
    load_layer += layer_loads(inputs, acts, 4 + 4 * col_tiles)
    for load in load_lists + load_layer + load_cur + load_pub:
        load.start()

    row = lax.broadcasted_iota(jnp.int32, (SUBLANES, TILE), 0)
    lane = lax.broadcasted_iota(jnp.int32, (SUBLANES, TILE), 1)
    for load in load_lists:
        load.wait()
    own_map = jnp.full((SUBLANES, TILE), slots, jnp.int32)
    for r in range(rounds):
        for s in range(slots):
            used = jnp.full((SUBLANES, TILE), counts[0, 0, r], jnp.int32) > s
            own_map = jnp.where((row == r) & (lane == ids[0, 0, r, s]) & used, s, own_map)
    maps[0] = own_map
    for r in range(rounds):
        sends[r][slots] = jnp.zeros((TILE, TILE), jnp.float32)
    for held in wide_recvs + narrow_recvs[:-1]:
        for side in range(NEAR):
            held[side, slots] = jnp.zeros((TILE, TILE), jnp.float32)

    for tile in range(row_tiles * col_tiles):
        places[0, tile] = tile // col_tiles
        places[1, tile] = tile % col_tiles

    map_copies = [
        pltpu.make_async_remote_copy(
            src_ref=maps.at[0], dst_ref=maps.at[1 + side], send_sem=map_send.at[side],
            recv_sem=map_recv.at[side], device_id=partners[side], device_id_type=MESH,
        )
        for side in range(SIDES)
    ]

    def slot_copy(r, side, first, size):
        recvs = narrow_recvs if side < NEAR else wide_recvs
        return pltpu.make_async_remote_copy(
            src_ref=sends[r].at[pl.ds(first, size)],
            dst_ref=recvs[r].at[side % NEAR, pl.ds(first, size)],
            send_sem=send_sem.at[r, side], recv_sem=recv_sem.at[r, side],
            device_id=partners[side], device_id_type=MESH,
        )

    def arrived(held, first_side, r, tile):
        total = held[r][0, map_table[1 + first_side, r, tile]]
        for side in range(1, NEAR):
            total = total + held[r][side, map_table[1 + first_side + side, r, tile]]
        return total

    def gradient(i, j):
        return lax.dot_general(
            acts[i], cots[j], (((0,), (0,)), ((), ())), preferred_element_type=jnp.float32
        )

    def place(r, s):
        tile = ids[0, 0, r, s]
        return tile, places[0, tile], places[1, tile]

    for load in load_layer:
        load.wait()
    for s in range(slots):
        _, i, j = place(0, s)
        sends[0][s] = LEARN_RATE * gradient(i, j)
    for load in load_cur + load_pub:
        load.wait()
    for load in load_mix:
        load.start()

    for r in range(rounds):
        for s in range(slots):
            tile, i, j = place(r, s)
            if r == 0:
                value = cur[i, j] - sends[r][s]
            else:
                value = cur[i, j] + CONSENSUS * NEIGHBOUR_WEIGHT * arrived(narrow_recvs, 0, r - 1, tile)
            sends[r][s] = value - pub[i, j]
            if r == 0 and s == 0:
                pl.semaphore_wait(barrier, SIDES)
                for copy in map_copies:
                    copy.start()
            for side in range(SIDES):
                slot_copy(r, side, s, 1).start()

        if r == 0:
            for copy in map_copies:
                copy.wait()
            table = pltpu.make_async_copy(maps, map_table, table_sem)
            table.start()
            table.wait()
            for load in load_mix:
                load.wait()

            def gradient_step(i, carry):
                for j in range(col_tiles):
                    cur[i, j] = cur[i, j] - LEARN_RATE * gradient(i, j)
                return carry

            lax.fori_loop(0, row_tiles, gradient_step, 0)

        for j in range(col_tiles):
            def own_part(i, carry):
                tile = i * col_tiles + j
                q = sends[r][map_table[0, r, tile]]
                new_pub = pub[i, j] + q
                new_cur, new_mix = cur[i, j], mix[i, j]
                if r:
                    total = arrived(narrow_recvs, 0, r - 1, tile)
                    new_cur = new_cur + CONSENSUS * NEIGHBOUR_WEIGHT * total
                    q = q + total
                new_mix = new_mix + NEIGHBOUR_WEIGHT * q
                pub[i, j] = new_pub
                mix[i, j] = new_mix
                cur[i, j] = new_cur + CONSENSUS * (new_mix - new_pub)
                return carry

            lax.fori_loop(0, row_tiles, own_part, 0)

        for side in range(NEAR, SIDES):
            slot_copy(r, side, 0, slots).wait_recv()

        def wide_part(i, carry):
            for j in range(col_tiles):
                total = arrived(wide_recvs, NEAR, r, i * col_tiles + j)
                mix[i, j] = mix[i, j] + NEIGHBOUR_WEIGHT * total
                cur[i, j] = cur[i, j] + CONSENSUS * NEIGHBOUR_WEIGHT * total
            return carry

        lax.fori_loop(0, row_tiles, wide_part, 0)

        if r == rounds - 1:
            writes = [
                pltpu.make_async_copy(held, target, out_sem.at[n])
                for n, (held, target) in enumerate(
                    ((cur, cur_out), (pub, pub_out), (mix, mix_out), (maps, maps_out))
                )
            ]
            for write in writes:
                write.start()
        for side in range(NEAR):
            slot_copy(r, side, 0, slots).wait_recv()

    for r in range(rounds):
        for side in range(SIDES):
            slot_copy(r, side, 0, slots).wait_send()
    for write in writes:
        write.wait()


def finish(
    last, table_in, cur, pub, mix, arrivals, params_out, public_out, mixed_out,
    table, new_cur, new_mix, table_sem, pub_sem, out_sem
):
    row_tiles, col_tiles = cur.shape[:2]
    slots = arrivals.shape[1]
    load = pltpu.make_async_copy(table_in, table, table_sem)
    load.start()
    copies = [
        pltpu.make_async_copy(
            pub.at[:, j], public_out.at[:, :, pl.ds(j * TILE, TILE)], pub_sem.at[j]
        )
        for j in range(col_tiles)
    ]
    for copy in copies:
        copy.start()
    load.wait()

    def writes(i):
        return (
            pltpu.make_async_copy(new_cur.at[i], params_out.at[i], out_sem.at[0, i]),
            pltpu.make_async_copy(new_mix.at[i], mixed_out.at[i], out_sem.at[1, i]),
        )

    def one_band(i, carry):
        for j in range(col_tiles):
            total = jnp.zeros((TILE, TILE), jnp.float32)
            for side in range(NEAR):
                slot = table[1 + side, last, i * col_tiles + j]
                part = arrivals[side, jnp.minimum(slot, slots - 1)]
                total = total + jnp.where(slot < slots, part, 0.0)
            span = slice(j * TILE, (j + 1) * TILE)
            new_cur[i, :, span] = cur[i, j] + CONSENSUS * NEIGHBOUR_WEIGHT * total
            new_mix[i, :, span] = mix[i, j] + NEIGHBOUR_WEIGHT * total
        for write in writes(i):
            write.start()
        return carry

    def drain(i, carry):
        for write in writes(i):
            write.wait()
        return carry

    lax.fori_loop(0, row_tiles, one_band, 0)
    lax.fori_loop(0, row_tiles, drain, 0)
    for copy in copies:
        copy.wait()


def solution(mesh):
    sizes = (mesh.shape["wide"], mesh.shape["narrow"])

    def on_device(params, public, mixed, inputs, cotangent, block_ids, block_counts):
        rounds, slots = block_ids.shape[2:]
        rows, cols = params.shape[2:]
        tokens = inputs.shape[2]
        col_tiles = cols // TILE
        banded = (rows // TILE, TILE, cols)
        held = pltpu.VMEM((rows // TILE, col_tiles, TILE, TILE), jnp.float32)
        any_spec = pl.BlockSpec(memory_space=pl.ANY)
        row_tiles = rows // TILE
        tiled = jax.ShapeDtypeStruct((row_tiles, col_tiles, TILE, TILE), jnp.float32)
        maps_shape = (1 + SIDES, SUBLANES, TILE)
        slots_shape = (NEAR, slots, TILE, TILE)
        cur, pub, mix, table, arrivals = pl.pallas_call(
            functools.partial(kernel, sizes, rounds, slots),
            out_shape=(
                tiled, tiled, tiled,
                jax.ShapeDtypeStruct(maps_shape, jnp.int32),
                jax.ShapeDtypeStruct(slots_shape, jnp.float32),
            ),
            in_specs=[any_spec] * 7,
            out_specs=(any_spec,) * 5,
            scratch_shapes=[
                pltpu.SMEM(block_ids.shape, jnp.int32),
                pltpu.SMEM(block_counts.shape, jnp.int32),
                pltpu.VMEM((row_tiles, tokens, TILE), inputs.dtype),
                pltpu.VMEM((col_tiles, tokens, TILE), cotangent.dtype),
                held, held, held,
                pltpu.SMEM((2, row_tiles * col_tiles), jnp.int32),
                pltpu.VMEM(maps_shape, jnp.int32),
                pltpu.SMEM(maps_shape, jnp.int32),
                pltpu.SemaphoreType.DMA((4 + 4 * col_tiles + row_tiles,)),
                pltpu.SemaphoreType.DMA((SIDES,)),
                pltpu.SemaphoreType.DMA((SIDES,)),
                pltpu.SemaphoreType.DMA,
                pltpu.SemaphoreType.DMA((rounds, SIDES)),
                pltpu.SemaphoreType.DMA((rounds, SIDES)),
                pltpu.SemaphoreType.DMA((4,)),
            ]
            + [pltpu.VMEM((slots + 1, TILE, TILE), jnp.float32)] * rounds
            + [pltpu.VMEM((NEAR, slots + 1, TILE, TILE), jnp.float32)] * (2 * rounds - 1),
            compiler_params=pltpu.CompilerParams(
                collective_id=0, has_side_effects=True, vmem_limit_bytes=LIMIT
            ),
            cost_estimate=pl.CostEstimate(
                flops=2 * tokens * rows * cols, bytes_accessed=6 * 4 * rows * cols, transcendentals=0
            ),
        )(
            in_hbm(block_ids), in_hbm(block_counts),
            *(in_hbm(x.reshape(banded)) for x in (params, public, mixed)),
            in_hbm(inputs), in_hbm(cotangent),
        )
        vmem_spec = pl.BlockSpec(memory_space=pltpu.VMEM)
        outs = pl.pallas_call(
            functools.partial(finish, rounds - 1),
            out_shape=(jax.ShapeDtypeStruct(banded, jnp.float32),) * 3,
            in_specs=[any_spec, vmem_spec, any_spec, vmem_spec, vmem_spec],
            out_specs=(any_spec,) * 3,
            scratch_shapes=[
                pltpu.SMEM(maps_shape, jnp.int32),
                pltpu.VMEM(banded, jnp.float32),
                pltpu.VMEM(banded, jnp.float32),
                pltpu.SemaphoreType.DMA,
                pltpu.SemaphoreType.DMA((col_tiles,)),
                pltpu.SemaphoreType.DMA((2, row_tiles)),
            ],
            compiler_params=pltpu.CompilerParams(vmem_limit_bytes=LIMIT),
            cost_estimate=pl.CostEstimate(
                flops=8 * rows * cols, bytes_accessed=8 * 4 * rows * cols, transcendentals=0
            ),
        )(table, in_vmem(cur), pub, in_vmem(mix), in_vmem(arrivals))
        return tuple(out.reshape(params.shape) for out in outs)

    spec = P("wide", "narrow", None, None)
    return jax.shard_map(
        on_device, mesh=mesh, in_specs=(spec,) * 6 + (P("wide", "narrow", None),),
        out_specs=(spec,) * 3, check_vma=False,
    )
```

```python
import functools

import jax
import jax.numpy as jnp
from jax import lax
from jax.experimental import pallas as pl
from jax.experimental.pallas import tpu as pltpu
from jax.sharding import PartitionSpec as P

TILE = 128
LEARN_RATE = 0.05
NEIGHBOUR_WEIGHT = 0.2
CONSENSUS = 0.4
LIMIT = 24 * 1024 * 1024
SUBLANES = 8
SIDES = 4
NEAR = 2
MESH = pl.DeviceIdType.MESH


def in_hbm(x):
    return pltpu.with_memory_space_constraint(x, pltpu.HBM)


def in_vmem(x):
    return pltpu.with_memory_space_constraint(x, pltpu.VMEM)


def kernel(
    sizes, rounds, slots, ids_in, counts_in, params, public, mixed, inputs, cotangent,
    cur_out, pub_out, mix_out, maps_out, last_recv,
    ids, counts, acts, cots, cur, pub, mix, places, maps, map_table, load_sem, map_send, map_recv, table_sem,
    send_sem, recv_sem, out_sem, *buffers
):
    sends, wide_recvs = buffers[:rounds], buffers[rounds:2 * rounds]
    narrow_recvs = buffers[2 * rounds:] + (last_recv,)
    row_tiles, col_tiles = cur.shape[:2]
    wide, narrow = lax.axis_index("wide"), lax.axis_index("narrow")
    wide_size, narrow_size = sizes
    partners = (
        (wide, lax.rem(narrow + 1, narrow_size)),
        (wide, lax.rem(narrow + narrow_size - 1, narrow_size)),
        (lax.rem(wide + 1, wide_size), narrow),
        (lax.rem(wide + wide_size - 1, wide_size), narrow),
    )

    barrier = pltpu.get_barrier_semaphore()
    for partner in partners:
        pl.semaphore_signal(barrier, inc=1, device_id=partner, device_id_type=MESH)

    load_lists = [
        pltpu.make_async_copy(ids_in, ids, load_sem.at[2 + 3 * col_tiles]),
        pltpu.make_async_copy(counts_in, counts, load_sem.at[3 + 3 * col_tiles]),
    ]
    def column_loads(source, held, first):
        return [
            pltpu.make_async_copy(
                source.at[:, :, pl.ds(j * TILE, TILE)], held.at[:, j], load_sem.at[first + j]
            )
            for j in range(col_tiles)
        ]

    def layer_loads(source, held, first):
        return [
            pltpu.make_async_copy(
                source.at[0, 0, :, pl.ds(n * TILE, TILE)], held.at[n], load_sem.at[first + n]
            )
            for n in range(held.shape[0])
        ]

    load_cur = column_loads(params, cur, 0)
    load_pub = column_loads(public, pub, col_tiles)
    load_mix = column_loads(mixed, mix, 2 * col_tiles)
    load_layer = layer_loads(cotangent, cots, 4 + 3 * col_tiles)
    load_layer += layer_loads(inputs, acts, 4 + 4 * col_tiles)
    for load in load_lists + load_layer + load_cur + load_pub:
        load.start()

    row = lax.broadcasted_iota(jnp.int32, (SUBLANES, TILE), 0)
    lane = lax.broadcasted_iota(jnp.int32, (SUBLANES, TILE), 1)
    for load in load_lists:
        load.wait()
    own_map = jnp.full((SUBLANES, TILE), slots, jnp.int32)
    for r in range(rounds):
        for s in range(slots):
            used = jnp.full((SUBLANES, TILE), counts[0, 0, r], jnp.int32) > s
            own_map = jnp.where((row == r) & (lane == ids[0, 0, r, s]) & used, s, own_map)
    maps[0] = own_map
    for r in range(rounds):
        sends[r][slots] = jnp.zeros((TILE, TILE), jnp.float32)
    for held in wide_recvs + narrow_recvs[:-1]:
        for side in range(NEAR):
            held[side, slots] = jnp.zeros((TILE, TILE), jnp.float32)

    for tile in range(row_tiles * col_tiles):
        places[0, tile] = tile // col_tiles
        places[1, tile] = tile % col_tiles

    map_copies = [
        pltpu.make_async_remote_copy(
            src_ref=maps.at[0], dst_ref=maps.at[1 + side], send_sem=map_send.at[side],
            recv_sem=map_recv.at[side], device_id=partners[side], device_id_type=MESH,
        )
        for side in range(SIDES)
    ]

    def slot_copy(r, side, first, size):
        recvs = narrow_recvs if side < NEAR else wide_recvs
        return pltpu.make_async_remote_copy(
            src_ref=sends[r].at[pl.ds(first, size)],
            dst_ref=recvs[r].at[side % NEAR, pl.ds(first, size)],
            send_sem=send_sem.at[r, side], recv_sem=recv_sem.at[r, side],
            device_id=partners[side], device_id_type=MESH,
        )

    def arrived(held, first_side, r, tile):
        total = held[r][0, map_table[1 + first_side, r, tile]]
        for side in range(1, NEAR):
            total = total + held[r][side, map_table[1 + first_side + side, r, tile]]
        return total

    def gradient(i, j):
        return lax.dot_general(
            acts[i], cots[j], (((0,), (0,)), ((), ())), preferred_element_type=jnp.float32
        )

    def place(r, s):
        tile = ids[0, 0, r, s]
        return tile, places[0, tile], places[1, tile]

    for load in load_layer:
        load.wait()
    for s in range(slots):
        _, i, j = place(0, s)
        sends[0][s] = LEARN_RATE * gradient(i, j)
    for load in load_cur + load_pub:
        load.wait()
    for load in load_mix:
        load.start()

    for r in range(rounds):
        for s in range(slots):
            tile, i, j = place(r, s)
            if r == 0:
                value = cur[i, j] - sends[r][s]
            else:
                value = cur[i, j] + CONSENSUS * NEIGHBOUR_WEIGHT * arrived(narrow_recvs, 0, r - 1, tile)
            sends[r][s] = value - pub[i, j]
            if r == 0 and s == 0:
                pl.semaphore_wait(barrier, SIDES)
                for copy in map_copies:
                    copy.start()
            for side in range(SIDES):
                slot_copy(r, side, s, 1).start()

        if r == 0:
            for copy in map_copies:
                copy.wait()
            table = pltpu.make_async_copy(maps, map_table, table_sem)
            table.start()
            table.wait()
            for load in load_mix:
                load.wait()

            def gradient_step(i, carry):
                for j in range(col_tiles):
                    cur[i, j] = cur[i, j] - LEARN_RATE * gradient(i, j)
                return carry

            lax.fori_loop(0, row_tiles, gradient_step, 0)

        for j in range(col_tiles):
            def own_part(i, carry):
                tile = i * col_tiles + j
                q = sends[r][map_table[0, r, tile]]
                new_pub = pub[i, j] + q
                new_cur, new_mix = cur[i, j], mix[i, j]
                if r:
                    total = arrived(narrow_recvs, 0, r - 1, tile)
                    new_cur = new_cur + CONSENSUS * NEIGHBOUR_WEIGHT * total
                    q = q + total
                new_mix = new_mix + NEIGHBOUR_WEIGHT * q
                pub[i, j] = new_pub
                mix[i, j] = new_mix
                cur[i, j] = new_cur + CONSENSUS * (new_mix - new_pub)
                return carry

            lax.fori_loop(0, row_tiles, own_part, 0)

        for side in range(NEAR, SIDES):
            slot_copy(r, side, 0, slots).wait_recv()

        def wide_part(i, carry):
            for j in range(col_tiles):
                total = arrived(wide_recvs, NEAR, r, i * col_tiles + j)
                mix[i, j] = mix[i, j] + NEIGHBOUR_WEIGHT * total
                cur[i, j] = cur[i, j] + CONSENSUS * NEIGHBOUR_WEIGHT * total
            return carry

        lax.fori_loop(0, row_tiles, wide_part, 0)

        if r == rounds - 1:
            writes = [
                pltpu.make_async_copy(held, target, out_sem.at[n])
                for n, (held, target) in enumerate(
                    ((cur, cur_out), (mix, mix_out), (maps, maps_out))
                )
            ]
            writes += [
                pltpu.make_async_copy(
                    pub.at[:, j], pub_out.at[:, :, pl.ds(j * TILE, TILE)], out_sem.at[3 + j]
                )
                for j in range(col_tiles)
            ]
            for write in writes:
                write.start()
        for side in range(NEAR):
            slot_copy(r, side, 0, slots).wait_recv()

    for r in range(rounds):
        for side in range(SIDES):
            slot_copy(r, side, 0, slots).wait_send()
    for write in writes:
        write.wait()


def finish(
    last, table_in, cur, pub, mix, arrivals, params_out, public_out, mixed_out,
    table, new_cur, new_mix, table_sem, pub_sem, out_sem
):
    row_tiles, col_tiles = cur.shape[:2]
    slots = arrivals.shape[1]
    load = pltpu.make_async_copy(table_in, table, table_sem)
    load.start()
    copies = [
        pltpu.make_async_copy(pub.at[i], public_out.at[i], pub_sem.at[i])
        for i in range(row_tiles)
    ]
    for copy in copies:
        copy.start()
    load.wait()

    def writes(i):
        return (
            pltpu.make_async_copy(new_cur.at[i], params_out.at[i], out_sem.at[0, i]),
            pltpu.make_async_copy(new_mix.at[i], mixed_out.at[i], out_sem.at[1, i]),
        )

    def one_band(i, carry):
        for j in range(col_tiles):
            total = jnp.zeros((TILE, TILE), jnp.float32)
            for side in range(NEAR):
                slot = table[1 + side, last, i * col_tiles + j]
                part = arrivals[side, jnp.minimum(slot, slots - 1)]
                total = total + jnp.where(slot < slots, part, 0.0)
            span = slice(j * TILE, (j + 1) * TILE)
            new_cur[i, :, span] = cur[i, j] + CONSENSUS * NEIGHBOUR_WEIGHT * total
            new_mix[i, :, span] = mix[i, j] + NEIGHBOUR_WEIGHT * total
        for write in writes(i):
            write.start()
        return carry

    def drain(i, carry):
        for write in writes(i):
            write.wait()
        return carry

    lax.fori_loop(0, row_tiles, one_band, 0)
    lax.fori_loop(0, row_tiles, drain, 0)
    for copy in copies:
        copy.wait()


def solution(mesh):
    sizes = (mesh.shape["wide"], mesh.shape["narrow"])

    def on_device(params, public, mixed, inputs, cotangent, block_ids, block_counts):
        rounds, slots = block_ids.shape[2:]
        rows, cols = params.shape[2:]
        tokens = inputs.shape[2]
        col_tiles = cols // TILE
        banded = (rows // TILE, TILE, cols)
        held = pltpu.VMEM((rows // TILE, col_tiles, TILE, TILE), jnp.float32)
        any_spec = pl.BlockSpec(memory_space=pl.ANY)
        row_tiles = rows // TILE
        tiled = jax.ShapeDtypeStruct((row_tiles, col_tiles, TILE, TILE), jnp.float32)
        maps_shape = (1 + SIDES, SUBLANES, TILE)
        slots_shape = (NEAR, slots, TILE, TILE)
        cur, pub, mix, table, arrivals = pl.pallas_call(
            functools.partial(kernel, sizes, rounds, slots),
            out_shape=(
                tiled, jax.ShapeDtypeStruct(banded, jnp.float32), tiled,
                jax.ShapeDtypeStruct(maps_shape, jnp.int32),
                jax.ShapeDtypeStruct(slots_shape, jnp.float32),
            ),
            in_specs=[any_spec] * 7,
            out_specs=(any_spec,) * 5,
            scratch_shapes=[
                pltpu.SMEM(block_ids.shape, jnp.int32),
                pltpu.SMEM(block_counts.shape, jnp.int32),
                pltpu.VMEM((row_tiles, tokens, TILE), inputs.dtype),
                pltpu.VMEM((col_tiles, tokens, TILE), cotangent.dtype),
                held, held, held,
                pltpu.SMEM((2, row_tiles * col_tiles), jnp.int32),
                pltpu.VMEM(maps_shape, jnp.int32),
                pltpu.SMEM(maps_shape, jnp.int32),
                pltpu.SemaphoreType.DMA((4 + 4 * col_tiles + row_tiles,)),
                pltpu.SemaphoreType.DMA((SIDES,)),
                pltpu.SemaphoreType.DMA((SIDES,)),
                pltpu.SemaphoreType.DMA,
                pltpu.SemaphoreType.DMA((rounds, SIDES)),
                pltpu.SemaphoreType.DMA((rounds, SIDES)),
                pltpu.SemaphoreType.DMA((3 + col_tiles,)),
            ]
            + [pltpu.VMEM((slots + 1, TILE, TILE), jnp.float32)] * rounds
            + [pltpu.VMEM((NEAR, slots + 1, TILE, TILE), jnp.float32)] * (2 * rounds - 1),
            compiler_params=pltpu.CompilerParams(
                collective_id=0, has_side_effects=True, vmem_limit_bytes=LIMIT
            ),
            cost_estimate=pl.CostEstimate(
                flops=2 * tokens * rows * cols, bytes_accessed=6 * 4 * rows * cols, transcendentals=0
            ),
        )(
            in_hbm(block_ids), in_hbm(block_counts),
            *(in_hbm(x.reshape(banded)) for x in (params, public, mixed)),
            in_hbm(inputs), in_hbm(cotangent),
        )
        vmem_spec = pl.BlockSpec(memory_space=pltpu.VMEM)
        outs = pl.pallas_call(
            functools.partial(finish, rounds - 1),
            out_shape=(jax.ShapeDtypeStruct(banded, jnp.float32),) * 3,
            in_specs=[any_spec, vmem_spec, any_spec, vmem_spec, vmem_spec],
            out_specs=(any_spec,) * 3,
            scratch_shapes=[
                pltpu.SMEM(maps_shape, jnp.int32),
                pltpu.VMEM(banded, jnp.float32),
                pltpu.VMEM(banded, jnp.float32),
                pltpu.SemaphoreType.DMA,
                pltpu.SemaphoreType.DMA((row_tiles,)),
                pltpu.SemaphoreType.DMA((2, row_tiles)),
            ],
            compiler_params=pltpu.CompilerParams(vmem_limit_bytes=LIMIT),
            cost_estimate=pl.CostEstimate(
                flops=8 * rows * cols, bytes_accessed=8 * 4 * rows * cols, transcendentals=0
            ),
        )(table, in_vmem(cur), pub, in_vmem(mix), in_vmem(arrivals))
        return tuple(out.reshape(params.shape) for out in outs)

    spec = P("wide", "narrow", None, None)
    return jax.shard_map(
        on_device, mesh=mesh, in_specs=(spec,) * 6 + (P("wide", "narrow", None),),
        out_specs=(spec,) * 3, check_vma=False,
    )
```

```python
import functools

import jax
import jax.numpy as jnp
from jax import lax
from jax.experimental import pallas as pl
from jax.experimental.pallas import tpu as pltpu
from jax.sharding import PartitionSpec as P

TILE = 128
LEARN_RATE = 0.05
NEIGHBOUR_WEIGHT = 0.2
CONSENSUS = 0.4
LIMIT = 24 * 1024 * 1024
SUBLANES = 8
SIDES = 4
NEAR = 2
MESH = pl.DeviceIdType.MESH


def in_hbm(x):
    return pltpu.with_memory_space_constraint(x, pltpu.HBM)


def in_vmem(x):
    return pltpu.with_memory_space_constraint(x, pltpu.VMEM)


def kernel(
    sizes, rounds, slots, ids_in, counts_in, params, public, mixed, inputs, cotangent,
    cur_out, pub_out, mix_out, maps_out, last_recv,
    ids, counts, acts, cots, cur, pub, mix, places, maps, map_table, load_sem, map_send, map_recv, table_sem,
    send_sem, recv_sem, out_sem, *buffers
):
    sends, wide_recvs = buffers[:rounds], buffers[rounds:2 * rounds]
    narrow_recvs = buffers[2 * rounds:] + (last_recv,)
    row_tiles, col_tiles = cur.shape[:2]
    wide, narrow = lax.axis_index("wide"), lax.axis_index("narrow")
    wide_size, narrow_size = sizes
    partners = (
        (wide, lax.rem(narrow + 1, narrow_size)),
        (wide, lax.rem(narrow + narrow_size - 1, narrow_size)),
        (lax.rem(wide + 1, wide_size), narrow),
        (lax.rem(wide + wide_size - 1, wide_size), narrow),
    )

    barrier = pltpu.get_barrier_semaphore()
    for partner in partners:
        pl.semaphore_signal(barrier, inc=1, device_id=partner, device_id_type=MESH)

    load_lists = [
        pltpu.make_async_copy(ids_in, ids, load_sem.at[2 + 3 * col_tiles]),
        pltpu.make_async_copy(counts_in, counts, load_sem.at[3 + 3 * col_tiles]),
    ]
    def column_loads(source, held, first):
        return [
            pltpu.make_async_copy(
                source.at[:, :, pl.ds(j * TILE, TILE)], held.at[:, j], load_sem.at[first + j]
            )
            for j in range(col_tiles)
        ]

    def layer_loads(source, held, first):
        return [
            pltpu.make_async_copy(
                source.at[0, 0, :, pl.ds(n * TILE, TILE)], held.at[n], load_sem.at[first + n]
            )
            for n in range(held.shape[0])
        ]

    load_cur = column_loads(params, cur, 0)
    load_pub = column_loads(public, pub, col_tiles)
    load_mix = column_loads(mixed, mix, 2 * col_tiles)
    load_layer = layer_loads(cotangent, cots, 4 + 3 * col_tiles)
    load_layer += layer_loads(inputs, acts, 4 + 4 * col_tiles)
    for load in load_lists + load_layer + load_cur + load_pub:
        load.start()

    row = lax.broadcasted_iota(jnp.int32, (SUBLANES, TILE), 0)
    lane = lax.broadcasted_iota(jnp.int32, (SUBLANES, TILE), 1)
    for load in load_lists:
        load.wait()
    own_map = jnp.full((SUBLANES, TILE), slots, jnp.int32)
    for r in range(rounds):
        for s in range(slots):
            used = jnp.full((SUBLANES, TILE), counts[0, 0, r], jnp.int32) > s
            own_map = jnp.where((row == r) & (lane == ids[0, 0, r, s]) & used, s, own_map)
    maps[0] = own_map
    for r in range(rounds):
        sends[r][slots] = jnp.zeros((TILE, TILE), jnp.float32)
    for held in wide_recvs + narrow_recvs[:-1]:
        for side in range(NEAR):
            held[side, slots] = jnp.zeros((TILE, TILE), jnp.float32)

    for tile in range(row_tiles * col_tiles):
        places[0, tile] = tile // col_tiles
        places[1, tile] = tile % col_tiles

    map_copies = [
        pltpu.make_async_remote_copy(
            src_ref=maps.at[0], dst_ref=maps.at[1 + side], send_sem=map_send.at[side],
            recv_sem=map_recv.at[side], device_id=partners[side], device_id_type=MESH,
        )
        for side in range(SIDES)
    ]

    def slot_copy(r, side, first, size):
        recvs = narrow_recvs if side < NEAR else wide_recvs
        return pltpu.make_async_remote_copy(
            src_ref=sends[r].at[pl.ds(first, size)],
            dst_ref=recvs[r].at[side % NEAR, pl.ds(first, size)],
            send_sem=send_sem.at[r, side], recv_sem=recv_sem.at[r, side],
            device_id=partners[side], device_id_type=MESH,
        )

    def arrived(held, first_side, r, tile):
        total = held[r][0, map_table[1 + first_side, r, tile]]
        for side in range(1, NEAR):
            total = total + held[r][side, map_table[1 + first_side + side, r, tile]]
        return total

    def gradient(i, j):
        return lax.dot_general(
            acts[i], cots[j], (((0,), (0,)), ((), ())), preferred_element_type=jnp.float32
        )

    def place(r, s):
        tile = ids[0, 0, r, s]
        return tile, places[0, tile], places[1, tile]

    for load in load_layer:
        load.wait()
    early = (slots + 1) // 2
    for s in range(early):
        _, i, j = place(0, s)
        sends[0][s] = LEARN_RATE * gradient(i, j)
    for load in load_cur + load_pub:
        load.wait()
    for load in load_mix:
        load.start()

    for r in range(rounds):
        for s in range(slots):
            tile, i, j = place(r, s)
            if r == 0:
                value = cur[i, j] - (sends[r][s] if s < early else LEARN_RATE * gradient(i, j))
            else:
                value = cur[i, j] + CONSENSUS * NEIGHBOUR_WEIGHT * arrived(narrow_recvs, 0, r - 1, tile)
            sends[r][s] = value - pub[i, j]
            if r == 0 and s == 0:
                pl.semaphore_wait(barrier, SIDES)
                for copy in map_copies:
                    copy.start()
            for side in range(SIDES):
                slot_copy(r, side, s, 1).start()

        if r == 0:
            for copy in map_copies:
                copy.wait()
            table = pltpu.make_async_copy(maps, map_table, table_sem)
            table.start()
            table.wait()
            for load in load_mix:
                load.wait()

            def gradient_step(i, carry):
                for j in range(col_tiles):
                    cur[i, j] = cur[i, j] - LEARN_RATE * gradient(i, j)
                return carry

            lax.fori_loop(0, row_tiles, gradient_step, 0)

        for j in range(col_tiles):
            def own_part(i, carry):
                tile = i * col_tiles + j
                q = sends[r][map_table[0, r, tile]]
                new_pub = pub[i, j] + q
                new_cur, new_mix = cur[i, j], mix[i, j]
                if r:
                    total = arrived(narrow_recvs, 0, r - 1, tile)
                    new_cur = new_cur + CONSENSUS * NEIGHBOUR_WEIGHT * total
                    q = q + total
                new_mix = new_mix + NEIGHBOUR_WEIGHT * q
                pub[i, j] = new_pub
                mix[i, j] = new_mix
                cur[i, j] = new_cur + CONSENSUS * (new_mix - new_pub)
                return carry

            lax.fori_loop(0, row_tiles, own_part, 0)

        for side in range(NEAR, SIDES):
            slot_copy(r, side, 0, slots).wait_recv()

        def wide_part(i, carry):
            for j in range(col_tiles):
                total = arrived(wide_recvs, NEAR, r, i * col_tiles + j)
                mix[i, j] = mix[i, j] + NEIGHBOUR_WEIGHT * total
                cur[i, j] = cur[i, j] + CONSENSUS * NEIGHBOUR_WEIGHT * total
            return carry

        lax.fori_loop(0, row_tiles, wide_part, 0)

        if r == rounds - 1:
            writes = [
                pltpu.make_async_copy(held, target, out_sem.at[n])
                for n, (held, target) in enumerate(
                    ((cur, cur_out), (mix, mix_out), (maps, maps_out))
                )
            ]
            writes += [
                pltpu.make_async_copy(
                    pub.at[:, j], pub_out.at[:, :, pl.ds(j * TILE, TILE)], out_sem.at[3 + j]
                )
                for j in range(col_tiles)
            ]
            for write in writes:
                write.start()
        for side in range(NEAR):
            slot_copy(r, side, 0, slots).wait_recv()

    for r in range(rounds):
        for side in range(SIDES):
            slot_copy(r, side, 0, slots).wait_send()
    for write in writes:
        write.wait()


def finish(
    last, table_in, cur, pub, mix, arrivals, params_out, public_out, mixed_out,
    table, new_cur, new_mix, table_sem, pub_sem, out_sem
):
    row_tiles, col_tiles = cur.shape[:2]
    slots = arrivals.shape[1]
    load = pltpu.make_async_copy(table_in, table, table_sem)
    load.start()
    copies = [
        pltpu.make_async_copy(pub.at[i], public_out.at[i], pub_sem.at[i])
        for i in range(row_tiles)
    ]
    for copy in copies:
        copy.start()
    load.wait()

    def writes(i):
        return (
            pltpu.make_async_copy(new_cur.at[i], params_out.at[i], out_sem.at[0, i]),
            pltpu.make_async_copy(new_mix.at[i], mixed_out.at[i], out_sem.at[1, i]),
        )

    def one_band(i, carry):
        for j in range(col_tiles):
            total = jnp.zeros((TILE, TILE), jnp.float32)
            for side in range(NEAR):
                slot = table[1 + side, last, i * col_tiles + j]
                part = arrivals[side, jnp.minimum(slot, slots - 1)]
                total = total + jnp.where(slot < slots, part, 0.0)
            span = slice(j * TILE, (j + 1) * TILE)
            new_cur[i, :, span] = cur[i, j] + CONSENSUS * NEIGHBOUR_WEIGHT * total
            new_mix[i, :, span] = mix[i, j] + NEIGHBOUR_WEIGHT * total
        for write in writes(i):
            write.start()
        return carry

    def drain(i, carry):
        for write in writes(i):
            write.wait()
        return carry

    lax.fori_loop(0, row_tiles, one_band, 0)
    lax.fori_loop(0, row_tiles, drain, 0)
    for copy in copies:
        copy.wait()


def solution(mesh):
    sizes = (mesh.shape["wide"], mesh.shape["narrow"])

    def on_device(params, public, mixed, inputs, cotangent, block_ids, block_counts):
        rounds, slots = block_ids.shape[2:]
        rows, cols = params.shape[2:]
        tokens = inputs.shape[2]
        col_tiles = cols // TILE
        banded = (rows // TILE, TILE, cols)
        held = pltpu.VMEM((rows // TILE, col_tiles, TILE, TILE), jnp.float32)
        any_spec = pl.BlockSpec(memory_space=pl.ANY)
        row_tiles = rows // TILE
        tiled = jax.ShapeDtypeStruct((row_tiles, col_tiles, TILE, TILE), jnp.float32)
        maps_shape = (1 + SIDES, SUBLANES, TILE)
        slots_shape = (NEAR, slots, TILE, TILE)
        cur, pub, mix, table, arrivals = pl.pallas_call(
            functools.partial(kernel, sizes, rounds, slots),
            out_shape=(
                tiled, jax.ShapeDtypeStruct(banded, jnp.float32), tiled,
                jax.ShapeDtypeStruct(maps_shape, jnp.int32),
                jax.ShapeDtypeStruct(slots_shape, jnp.float32),
            ),
            in_specs=[any_spec] * 7,
            out_specs=(any_spec,) * 5,
            scratch_shapes=[
                pltpu.SMEM(block_ids.shape, jnp.int32),
                pltpu.SMEM(block_counts.shape, jnp.int32),
                pltpu.VMEM((row_tiles, tokens, TILE), inputs.dtype),
                pltpu.VMEM((col_tiles, tokens, TILE), cotangent.dtype),
                held, held, held,
                pltpu.SMEM((2, row_tiles * col_tiles), jnp.int32),
                pltpu.VMEM(maps_shape, jnp.int32),
                pltpu.SMEM(maps_shape, jnp.int32),
                pltpu.SemaphoreType.DMA((4 + 4 * col_tiles + row_tiles,)),
                pltpu.SemaphoreType.DMA((SIDES,)),
                pltpu.SemaphoreType.DMA((SIDES,)),
                pltpu.SemaphoreType.DMA,
                pltpu.SemaphoreType.DMA((rounds, SIDES)),
                pltpu.SemaphoreType.DMA((rounds, SIDES)),
                pltpu.SemaphoreType.DMA((3 + col_tiles,)),
            ]
            + [pltpu.VMEM((slots + 1, TILE, TILE), jnp.float32)] * rounds
            + [pltpu.VMEM((NEAR, slots + 1, TILE, TILE), jnp.float32)] * (2 * rounds - 1),
            compiler_params=pltpu.CompilerParams(
                collective_id=0, has_side_effects=True, vmem_limit_bytes=LIMIT
            ),
            cost_estimate=pl.CostEstimate(
                flops=2 * tokens * rows * cols, bytes_accessed=6 * 4 * rows * cols, transcendentals=0
            ),
        )(
            in_hbm(block_ids), in_hbm(block_counts),
            *(in_hbm(x.reshape(banded)) for x in (params, public, mixed)),
            in_hbm(inputs), in_hbm(cotangent),
        )
        vmem_spec = pl.BlockSpec(memory_space=pltpu.VMEM)
        outs = pl.pallas_call(
            functools.partial(finish, rounds - 1),
            out_shape=(jax.ShapeDtypeStruct(banded, jnp.float32),) * 3,
            in_specs=[any_spec, vmem_spec, any_spec, vmem_spec, vmem_spec],
            out_specs=(any_spec,) * 3,
            scratch_shapes=[
                pltpu.SMEM(maps_shape, jnp.int32),
                pltpu.VMEM(banded, jnp.float32),
                pltpu.VMEM(banded, jnp.float32),
                pltpu.SemaphoreType.DMA,
                pltpu.SemaphoreType.DMA((row_tiles,)),
                pltpu.SemaphoreType.DMA((2, row_tiles)),
            ],
            compiler_params=pltpu.CompilerParams(vmem_limit_bytes=LIMIT),
            cost_estimate=pl.CostEstimate(
                flops=8 * rows * cols, bytes_accessed=8 * 4 * rows * cols, transcendentals=0
            ),
        )(table, in_vmem(cur), pub, in_vmem(mix), in_vmem(arrivals))
        return tuple(out.reshape(params.shape) for out in outs)

    spec = P("wide", "narrow", None, None)
    return jax.shard_map(
        on_device, mesh=mesh, in_specs=(spec,) * 6 + (P("wide", "narrow", None),),
        out_specs=(spec,) * 3, check_vma=False,
    )
```
